32 devices in a mesh: row: 8 (over z, x), sub: 4 (over y, core).
Axes of the slice: x: 2, y: 2, z: 4, core: 2. Of those that a mesh axis runs over, the one named last changes fastest.
Arguments:
- feature_vectors: bfloat16 [2048, 1024], P('row'), may hold values from -6 to 6
- upstream_sensitivity: bfloat16 [2048, 1024], P('row'), may hold values from -0.4375 to 0.4375
- linear_mapping_matrix: bfloat16 [1024, 1024], P(None, 'sub'), may hold values from -0.1875 to 0.1875
- centroid_tables: float32 [128, 8, 256], P('sub'), may hold values from -6 to 6
- softness_factor: float32 [128], P('sub'), may hold values from 0.01 to 8
Outputs:
- input_grad: bfloat16 [2048, 1024], P('row', 'sub')
- rotation_grad: float32 [1024, 1024], P('row', 'sub')
- centroid_table_derivative: float32 [128, 8, 256], P('sub')
The draws below stay inside these ranges and needn't reach their ends.
All inputs are finite; a program needn't handle non-finite values.
Results may differ from the reference program's by a relative error of at most 0.018.
Values may be sent and summed in bfloat16 or wider, within the bound.
A program may use at most 64 MiB of HBM per device.

```python
import jax
import jax.numpy as jnp
from jax import lax

D = 1024
M = 128
K = 256
DSUB = 8
ROWS = 2048
N_SUB = 4


def draw_softness_factor(key, part):
    key = jax.random.fold_in(key, 7)
    first = jax.random.fold_in(key, 0)
    spread = jax.random.uniform(first, (M,), jnp.float32, jnp.log(0.5), jnp.log(8.0))
    values = jnp.exp(spread)
    return values.astype(jnp.float32)


def strengthened(array, stream_key, source, target, parts, factor):
    owner, partner = [(jnp.arange(array.shape[axis_at]) // (array.shape[axis_at] // parts)).reshape([-1 if axis == axis_at else 1 for axis in range(array.ndim)]) for axis_at in (source, target)]
    chosen = jax.random.permutation(stream_key, parts)[partner]
    strong = (owner == chosen) | (owner == (partner + parts // 2) % parts)
    return jnp.where(strong, factor * array, array)


def level_of(rng, dims, cuts, low, high):
    factor_of, own = 1.0, jax.random.fold_in(rng, 6)
    for position, blocks in cuts:
        steps = jnp.exp(jax.random.uniform(jax.random.fold_in(own, position), (blocks,), jnp.float32, low / len(cuts), high / len(cuts)))
        factor_of = factor_of * jnp.repeat(steps, dims[position] // blocks).reshape([-1 if axis == position else 1 for axis in range(len(dims))])
    return factor_of


def scatter_about(stream_key, extent, scale, limit, cuts=(), held_as=jnp.bfloat16):
    values = jax.random.normal(stream_key, extent, jnp.float32) * scale
    if len(cuts) > 0:
        values = level_of(stream_key, extent, cuts, -0.22, 0.18) * values
    return jnp.clip(values, min=-limit, max=limit).astype(held_as)


def heavy_noise(stream_key, shape, deviation, reach, cuts, heavy, dtype=jnp.bfloat16):
    entries = deviation * jax.random.normal(stream_key, shape, jnp.float32)
    if cuts:
        entries = entries * level_of(stream_key, shape, cuts, -0.22, 0.18)
    return jnp.clip(strengthened(entries, jax.random.fold_in(stream_key, 3), *heavy), -reach, reach).astype(dtype)


def setup_inputs(seed: int = 0) -> dict:
    key_list = jax.random.split(jax.random.key(seed), 6)
    feature_vectors = scatter_about(key_list[0], (ROWS, D), 1.0, 6.0, ((0, 8),))
    upstream_sensitivity = heavy_noise(key_list[1], (ROWS, D), 0.02, 0.4375, ((0, 8),), (0, 1, 8, 2.0))
    linear_mapping_matrix = scatter_about(key_list[2], (D, D), D ** -0.5, 0.1875, ((1, 4),))
    centroid_tables = scatter_about(key_list[3], (M, DSUB, K), 1.0, 6.0, ((0, 4),), jnp.float32)
    softness_factor = draw_softness_factor(jax.random.fold_in(key_list[5], 71), 0)
    return dict(feature_vectors=feature_vectors, upstream_sensitivity=upstream_sensitivity, linear_mapping_matrix=linear_mapping_matrix, centroid_tables=centroid_tables, softness_factor=softness_factor)


def subspace(rotated, recon_grad, centers, temper):
    highest = lax.Precision.HIGHEST
    inner_term = jnp.dot(rotated, centers, precision=highest)
    distance = jnp.sum(rotated * rotated, 1, keepdims=True) - 2.0 * inner_term + jnp.sum(centers * centers, 0)[None, :]
    scores = -distance / temper
    assign = jax.nn.softmax(scores, axis=-1)
    quantized_approximation = jnp.dot(assign, centers.T, precision=highest)
    prob_grad = jnp.dot(recon_grad, centers, precision=highest)
    score_grad = assign * (prob_grad - jnp.sum(assign * prob_grad, 1, keepdims=True))
    weighted = score_grad * (2.0 / temper)
    turned_derivative = jnp.dot(weighted, centers.T, precision=highest) - rotated * jnp.sum(weighted, 1, keepdims=True)
    center_grad = jnp.dot(recon_grad.T, assign, precision=highest) + jnp.dot(rotated.T, weighted, precision=highest) - centers * jnp.sum(weighted, 0)[None, :]
    return quantized_approximation, turned_derivative, center_grad


def reference(feature_vectors, upstream_sensitivity, linear_mapping_matrix, centroid_tables, softness_factor):
    rotated = jnp.dot(feature_vectors, linear_mapping_matrix, preferred_element_type=jnp.float32)
    recon_grad = jnp.dot(upstream_sensitivity, linear_mapping_matrix, preferred_element_type=jnp.float32)
    turned_segments = rotated.reshape(ROWS, M, DSUB).transpose(1, 0, 2)
    derivative_blocks_list = recon_grad.reshape(ROWS, M, DSUB).transpose(1, 0, 2)

    def lone_partition_index(packed):
        return subspace(packed[0], packed[1], packed[2], packed[3])

    quantized_approximation, turned_derivative, centroid_table_derivative = lax.map(lone_partition_index, (turned_segments, derivative_blocks_list, centroid_tables, softness_factor))
    recon_low = quantized_approximation.transpose(1, 0, 2).reshape(ROWS, D).astype(jnp.bfloat16)
    grad_low = turned_derivative.transpose(1, 0, 2).reshape(ROWS, D).astype(jnp.bfloat16)
    rotation_grad = jnp.dot(feature_vectors.T, grad_low, preferred_element_type=jnp.float32) + jnp.dot(upstream_sensitivity.T, recon_low, preferred_element_type=jnp.float32)
    width = D // N_SUB
    total = jnp.zeros((ROWS, D), jnp.float32)
    for block in range(N_SUB):
        term = jnp.dot(grad_low[:, block * width:(block + 1) * width], linear_mapping_matrix[:, block * width:(block + 1) * width].T, preferred_element_type=jnp.float32)
        term = lax.optimization_barrier(term.astype(jnp.bfloat16))
        total = total + term.astype(jnp.float32)
    return total.astype(jnp.bfloat16), rotation_grad, centroid_table_derivative
```

```python
import functools

import jax
import jax.numpy as jnp
from jax import lax
from jax.experimental import pallas as pl
from jax.experimental.pallas import tpu as pltpu
from jax.sharding import PartitionSpec as P

MESH = pl.DeviceIdType.MESH
LOG2E = 1.4426950408889634
CHUNKS = 2
GROUP = 4
F32 = jnp.float32
BF16 = jnp.bfloat16


def nn(a, b):
    return lax.dot_general(a, b, (((1,), (0,)), ((), ())), preferred_element_type=F32)


def nt(a, b):
    return lax.dot_general(a, b, (((1,), (1,)), ((), ())), preferred_element_type=F32)


def low(x):
    return x.astype(BF16).astype(F32)


def split3(x):
    first = low(x)
    rest = x - first
    second = low(rest)
    return first, second, low(rest - second)


def split2(x):
    first = low(x)
    return first, low(x - first)


def for_peers(me, count, body):
    if count <= 8:
        for step in range(1, count):
            body(lax.rem(me + step, count))
    else:

        def run(step, carry):
            body(lax.rem(me + step, count))
            return carry

        lax.fori_loop(1, count, run, 0)


def subspaces(first, book_ref, temper_ref, turned_ref, slope_ref, grad_ref, recon_ref, cg_ref):
    width = 8
    codes = book_ref.shape[1]
    rows = turned_ref.shape[1]
    at = [pl.ds(pl.multiple_of((first + j) * width, width), width) for j in range(GROUP)]
    sub_k = lax.broadcasted_iota(jnp.int32, (width, codes), 0)
    sub_n = lax.broadcasted_iota(jnp.int32, (width, rows), 0)
    none_k = jnp.zeros((width, codes), F32)
    none_n = jnp.zeros((width, rows), F32)
    ones_n = jnp.where(sub_n < 3, 1.0, 0.0).astype(F32)
    one_k = jnp.where(sub_k == 0, 1.0, 0.0).astype(F32)
    both, books = [], []
    for j in range(GROUP):
        temper = temper_ref[first + j]
        c, z, g = book_ref[at[j], :], turned_ref[at[j], :], slope_ref[at[j], :]
        c1, c2, c3 = split3(c)
        square = jnp.sum(c * c, 0, keepdims=True) * (-LOG2E / jnp.full((1, codes), temper, F32))
        q1, q2, q3 = split3(square)
        squares = jnp.where(
            sub_k == 0, q1, jnp.where(sub_k == 1, q2, jnp.where(sub_k == 2, q3, 0.0))
        )
        left = jnp.concatenate([c1, c2, c3, c1, c2, c1, squares, none_k], 0).astype(BF16).T
        z1, z2, z3 = split3(z * (2.0 * LOG2E / jnp.full((1, rows), temper, F32)))
        g1, g2, g3 = split3(g)
        right = jnp.concatenate(
            [
                jnp.concatenate([z1, z1, z1, z2, z2, z3, ones_n, none_n], 0).astype(BF16),
                jnp.concatenate([g1, g1, g1, g2, g2, g3, none_n, none_n], 0).astype(BF16),
            ],
            1,
        )
        both.append(nn(left, right))
        books.append(jnp.concatenate([c1, c2, one_k, none_k], 0).astype(BF16))
    exps, exps_low = [], []
    for j in range(GROUP):
        s = both[j][:, :rows]
        e = jnp.exp2(s - jnp.max(s, 0, keepdims=True))
        exps.append(e)
        exps_low.append(e.astype(BF16))
    sums = [nn(books[j], exps_low[j]) for j in range(GROUP)]
    slopes, scales, backs = [], [], []
    for j in range(GROUP):
        back = 1.0 / sums[j][16:17]
        recon = (sums[j][0:8] + sums[j][8:16]) * back
        recon_ref[at[j], :] = recon
        mean = jnp.sum(slope_ref[at[j], :] * recon, 0, keepdims=True)
        slopes.append((exps[j] * (both[j][:, rows:] - mean)).astype(BF16))
        backs.append(back)
        scales.append(back * (2.0 / jnp.full((1, rows), temper_ref[first + j], F32)))
    for j in range(GROUP):
        c, z, g = book_ref[at[j], :], turned_ref[at[j], :], slope_ref[at[j], :]
        w = nn(books[j], slopes[j])
        total = w[16:17] * scales[j]
        grad_ref[at[j], :] = (w[0:8] + w[8:16]) * scales[j] - z * total
        a1, a2 = split2(g * backs[j])
        b1, b2 = split2(z * scales[j])
        t1, t2 = split2(scales[j])
        tops = jnp.where(sub_n == 0, t1, jnp.where(sub_n == 1, t2, 0.0))
        from_assign = nt(jnp.concatenate([a1, a2], 0).astype(BF16), exps_low[j])
        from_weight = nt(jnp.concatenate([b1, b2, tops, none_n], 0).astype(BF16), slopes[j])
        cg_ref[at[j], :] = (
            (from_assign[0:8] + from_assign[8:16])
            + (from_weight[0:8] + from_weight[8:16])
            - c * (from_weight[16:17] + from_weight[17:18])
        )


def kernel(
    row_count,
    sub_count,
    share_codes,
    x_ref,
    u_ref,
    w_ref,
    book_ref,
    temper_ref,
    input_ref,
    rotation_ref,
    codes_ref,
    xt,
    ut,
    turned,
    slope,
    grad,
    recon,
    cg,
    grad_low,
    in_out,
    in_got,
    rot_out,
    rot_got,
    cg_out,
    cg_got,
    cg_sum,
    cg_all,
    in_send,
    in_recv,
    rot_send,
    rot_recv,
    cg_send,
    cg_recv,
    all_send,
    all_recv,
):
    row, sub = lax.axis_index("row"), lax.axis_index("sub")
    rows, features = x_ref.shape
    columns = w_ref.shape[1]
    span = columns // CHUNKS
    block = features // row_count
    slab = features // sub_count
    piece = span // row_count

    barrier = pltpu.get_barrier_semaphore()

    def greet_row(peer):
        pl.semaphore_signal(barrier, inc=1, device_id=(peer, sub), device_id_type=MESH)

    def greet_sub(peer):
        pl.semaphore_signal(barrier, inc=1, device_id=(row, peer), device_id_type=MESH)

    for_peers(row, row_count, greet_row)
    for_peers(sub, sub_count, greet_sub)

    turned[...] = nn(x_ref[...], w_ref[...]).T
    slope[...] = nn(u_ref[...], w_ref[...]).T
    xt[...] = x_ref[...].T
    ut[...] = u_ref[...].T

    def rot_copy(h, peer, slot):
        return pltpu.make_async_remote_copy(
            src_ref=rot_out.at[h, pl.ds(pl.multiple_of(peer * block, block), block)],
            dst_ref=rot_got.at[h, slot],
            send_sem=rot_send.at[h, peer],
            recv_sem=rot_recv.at[h, slot],
            device_id=(peer, sub),
            device_id_type=MESH,
        )

    def cg_copy(h, peer, slot):
        return pltpu.make_async_remote_copy(
            src_ref=cg_out.at[h, pl.ds(pl.multiple_of(peer * piece, piece), piece)],
            dst_ref=cg_got.at[h, slot],
            send_sem=cg_send.at[h, peer],
            recv_sem=cg_recv.at[h, slot],
            device_id=(peer, sub),
            device_id_type=MESH,
        )

    def all_copy(h, peer, slot):
        return pltpu.make_async_remote_copy(
            src_ref=cg_sum.at[h],
            dst_ref=cg_all.at[h, slot],
            send_sem=all_send.at[h, peer],
            recv_sem=all_recv.at[h, slot],
            device_id=(peer, sub),
            device_id_type=MESH,
        )

    def in_copy(peer, slot):
        return pltpu.make_async_remote_copy(
            src_ref=in_out.at[pl.ds(pl.multiple_of(peer * slab, slab), slab)],
            dst_ref=in_got.at[slot],
            send_sem=in_send.at[peer],
            recv_sem=in_recv.at[slot],
            device_id=(row, peer),
            device_id_type=MESH,
        )

    def work(h):
        per = span // 8

        def body(i, carry):
            subspaces(
                h * per + i * GROUP,
                book_ref,
                temper_ref,
                turned,
                slope,
                grad,
                recon,
                cg,
            )
            return carry

        lax.fori_loop(0, per // GROUP, body, 0)
        grad_low[pl.ds(h * span, span), :] = grad[pl.ds(h * span, span), :].astype(BF16)

    def send_codes(h):
        if share_codes:
            cg_out[h] = cg[pl.ds(h * span, span), :].astype(BF16)
            for_peers(row, row_count, lambda peer: cg_copy(h, peer, row).start())
        else:
            codes_ref[pl.ds(h * span, span), :] = cg[pl.ds(h * span, span), :]

    def send_rotation(h):
        rot_out[h] = (
            nt(xt[...], grad_low[pl.ds(h * span, span), :])
            + nt(ut[...], recon[pl.ds(h * span, span), :].astype(BF16))
        ).astype(BF16)
        for_peers(row, row_count, lambda peer: rot_copy(h, peer, row).start())

    def finish_codes(h):
        if share_codes:
            own = pl.ds(pl.multiple_of(row * piece, piece), piece)
            for_peers(row, row_count, lambda peer: cg_copy(h, row, peer).wait_recv())
            cg_got[h, row] = cg_out[h, own, :]
            total = cg_got[h, 0].astype(F32)
            for other in range(1, row_count):
                total += cg_got[h, other].astype(F32)
            cg_sum[h] = total.astype(BF16)
            for_peers(row, row_count, lambda peer: all_copy(h, peer, row).start())

    def finish_rotation(h):
        for_peers(row, row_count, lambda peer: rot_copy(h, row, peer).wait_recv())
        rot_got[h, row] = rot_out[h, pl.ds(pl.multiple_of(row * block, block), block), :]
        total = rot_got[h, 0].astype(F32)
        for other in range(1, row_count):
            total += rot_got[h, other].astype(F32)
        rotation_ref[:, pl.ds(h * span, span)] = total

    work(0)
    pl.semaphore_wait(barrier, row_count + sub_count - 2)
    send_codes(0)
    send_rotation(0)
    work(1)
    send_codes(1)
    in_out[...] = nn(w_ref[...], grad_low[...]).astype(BF16)
    for_peers(sub, sub_count, lambda peer: in_copy(peer, sub).start())
    send_rotation(1)
    finish_codes(0)
    finish_codes(1)
    finish_rotation(0)

    for_peers(sub, sub_count, lambda peer: in_copy(sub, peer).wait_recv())
    in_got[sub] = in_out[pl.ds(pl.multiple_of(sub * slab, slab), slab), :]
    total = in_got[0].astype(F32)
    for other in range(1, sub_count):
        total += in_got[other].astype(F32)
    input_ref[...] = total.T.astype(BF16)

    finish_rotation(1)

    if share_codes:
        for h in range(CHUNKS):
            for_peers(row, row_count, lambda peer: all_copy(h, row, peer).wait_recv())
            cg_all[h, row] = cg_sum[h]
            for other in range(row_count):
                codes_ref[pl.ds(h * span + other * piece, piece), :] = cg_all[h, other].astype(F32)

    for_peers(sub, sub_count, lambda peer: in_copy(peer, sub).wait_send())
    for h in range(CHUNKS):
        for_peers(row, row_count, lambda peer: rot_copy(h, peer, row).wait_send())
        if share_codes:
            for_peers(row, row_count, lambda peer: cg_copy(h, peer, row).wait_send())
            for_peers(row, row_count, lambda peer: all_copy(h, peer, row).wait_send())


def on_device(
    feature_vectors, upstream_sensitivity, linear_mapping_matrix, centroid_tables, softness_factor
):
    row_count, sub_count = lax.axis_size("row"), lax.axis_size("sub")
    rows, features = feature_vectors.shape
    columns = linear_mapping_matrix.shape[1]
    subs, width, codes = centroid_tables.shape
    span = columns // CHUNKS
    block = features // row_count
    slab = features // sub_count
    share_codes = span % (16 * row_count) == 0
    piece = span // row_count if share_codes else 16
    row_sems = pltpu.SemaphoreType.DMA((CHUNKS, row_count))
    sub_sems = pltpu.SemaphoreType.DMA((sub_count,))
    vmem = pl.BlockSpec(memory_space=pltpu.VMEM)
    input_grad, rotation_grad, code_grad = pl.pallas_call(
        functools.partial(kernel, row_count, sub_count, share_codes),
        out_shape=(
            jax.ShapeDtypeStruct((rows, slab), BF16),
            jax.ShapeDtypeStruct((block, columns), F32),
            jax.ShapeDtypeStruct((subs * width, codes), F32),
        ),
        in_specs=[vmem, vmem, vmem, vmem, pl.BlockSpec(memory_space=pltpu.SMEM)],
        out_specs=(vmem, vmem, vmem),
        scratch_shapes=[
            pltpu.VMEM((features, rows), BF16),
            pltpu.VMEM((features, rows), BF16),
            pltpu.VMEM((columns, rows), F32),
            pltpu.VMEM((columns, rows), F32),
            pltpu.VMEM((columns, rows), F32),
            pltpu.VMEM((columns, rows), F32),
            pltpu.VMEM((columns, codes), F32),
            pltpu.VMEM((columns, rows), BF16),
            pltpu.VMEM((features, rows), BF16),
            pltpu.VMEM((sub_count, slab, rows), BF16),
            pltpu.VMEM((CHUNKS, features, span), BF16),
            pltpu.VMEM((CHUNKS, row_count, block, span), BF16),
            pltpu.VMEM((CHUNKS, span, codes), BF16),
            pltpu.VMEM((CHUNKS, row_count, piece, codes), BF16),
            pltpu.VMEM((CHUNKS, piece, codes), BF16),
            pltpu.VMEM((CHUNKS, row_count, piece, codes), BF16),
            sub_sems,
            sub_sems,
            row_sems,
            row_sems,
            row_sems,
            row_sems,
            row_sems,
            row_sems,
        ],
        compiler_params=pltpu.CompilerParams(
            collective_id=0, has_side_effects=True, vmem_limit_bytes=48 * 1024 * 1024
        ),
        name="soft_pq_backward",
    )(
        feature_vectors,
        upstream_sensitivity,
        linear_mapping_matrix,
        centroid_tables.reshape(subs * width, codes),
        softness_factor,
    )
    if not share_codes:
        code_grad = lax.psum(code_grad, "row")
    return input_grad, rotation_grad, code_grad.reshape(subs, width, codes)


def solution(mesh):
    return jax.shard_map(
        on_device,
        mesh=mesh,
        in_specs=(P("row", None), P("row", None), P(None, "sub"), P("sub", None, None), P("sub")),
        out_specs=(P("row", "sub"), P("row", "sub"), P("sub", None, None)),
        check_vma=False,
    )
```

```python
import functools

import jax
import jax.numpy as jnp
from jax import lax
from jax.experimental import pallas as pl
from jax.experimental.pallas import tpu as pltpu
from jax.sharding import PartitionSpec as P

MESH = pl.DeviceIdType.MESH
LOG2E = 1.4426950408889634
CHUNKS = 4
GROUP = 4
F32 = jnp.float32
BF16 = jnp.bfloat16


def nn(a, b):
    return lax.dot_general(a, b, (((1,), (0,)), ((), ())), preferred_element_type=F32)


def nt(a, b):
    return lax.dot_general(a, b, (((1,), (1,)), ((), ())), preferred_element_type=F32)


def low(x):
    return x.astype(BF16).astype(F32)


def split3(x):
    first = low(x)
    rest = x - first
    second = low(rest)
    return first, second, low(rest - second)


def split2(x):
    first = low(x)
    return first, low(x - first)


def for_peers(me, count, body):
    if count <= 8:
        for step in range(1, count):
            body(lax.rem(me + step, count))
    else:

        def run(step, carry):
            body(lax.rem(me + step, count))
            return carry

        lax.fori_loop(1, count, run, 0)


def subspaces(first, book_ref, temper_ref, turned_ref, slope_ref, grad_ref, recon_ref, cg_ref):
    width = 8
    codes = book_ref.shape[1]
    rows = turned_ref.shape[1]
    at = [pl.ds(pl.multiple_of((first + j) * width, width), width) for j in range(GROUP)]
    sub_k = lax.broadcasted_iota(jnp.int32, (width, codes), 0)
    sub_n = lax.broadcasted_iota(jnp.int32, (width, rows), 0)
    none_k = jnp.zeros((width, codes), F32)
    none_n = jnp.zeros((width, rows), F32)
    ones_n = jnp.where(sub_n < 3, 1.0, 0.0).astype(F32)
    one_k = jnp.where(sub_k == 0, 1.0, 0.0).astype(F32)
    both, books = [], []
    for j in range(GROUP):
        temper = temper_ref[first + j]
        c, z, g = book_ref[at[j], :], turned_ref[at[j], :], slope_ref[at[j], :]
        c1, c2, c3 = split3(c)
        square = jnp.sum(c * c, 0, keepdims=True) * (-LOG2E / jnp.full((1, codes), temper, F32))
        q1, q2, q3 = split3(square)
        squares = jnp.where(
            sub_k == 0, q1, jnp.where(sub_k == 1, q2, jnp.where(sub_k == 2, q3, 0.0))
        )
        left = jnp.concatenate([c1, c2, c3, c1, c2, c1, squares, none_k], 0).astype(BF16).T
        z1, z2, z3 = split3(z * (2.0 * LOG2E / jnp.full((1, rows), temper, F32)))
        g1, g2, g3 = split3(g)
        right = jnp.concatenate(
            [
                jnp.concatenate([z1, z1, z1, z2, z2, z3, ones_n, none_n], 0).astype(BF16),
                jnp.concatenate([g1, g1, g1, g2, g2, g3, none_n, none_n], 0).astype(BF16),
            ],
            1,
        )
        both.append(nn(left, right))
        books.append(jnp.concatenate([c1, c2, one_k, none_k], 0).astype(BF16))
    exps, exps_low = [], []
    for j in range(GROUP):
        s = both[j][:, :rows]
        e = jnp.exp2(s - jnp.max(s, 0, keepdims=True))
        exps.append(e)
        exps_low.append(e.astype(BF16))
    sums = [nn(books[j], exps_low[j]) for j in range(GROUP)]
    slopes, scales, backs = [], [], []
    for j in range(GROUP):
        back = 1.0 / sums[j][16:17]
        recon = (sums[j][0:8] + sums[j][8:16]) * back
        recon_ref[at[j], :] = recon
        mean = jnp.sum(slope_ref[at[j], :] * recon, 0, keepdims=True)
        slopes.append((exps[j] * (both[j][:, rows:] - mean)).astype(BF16))
        backs.append(back)
        scales.append(back * (2.0 / jnp.full((1, rows), temper_ref[first + j], F32)))
    for j in range(GROUP):
        c, z, g = book_ref[at[j], :], turned_ref[at[j], :], slope_ref[at[j], :]
        w = nn(books[j], slopes[j])
        total = w[16:17] * scales[j]
        grad_ref[at[j], :] = (w[0:8] + w[8:16]) * scales[j] - z * total
        a1, a2 = split2(g * backs[j])
        b1, b2 = split2(z * scales[j])
        t1, t2 = split2(scales[j])
        tops = jnp.where(sub_n == 0, t1, jnp.where(sub_n == 1, t2, 0.0))
        from_assign = nt(jnp.concatenate([a1, a2], 0).astype(BF16), exps_low[j])
        from_weight = nt(jnp.concatenate([b1, b2, tops, none_n], 0).astype(BF16), slopes[j])
        cg_ref[at[j], :] = (
            (from_assign[0:8] + from_assign[8:16])
            + (from_weight[0:8] + from_weight[8:16])
            - c * (from_weight[16:17] + from_weight[17:18])
        )


def kernel(
    row_count,
    sub_count,
    share,
    x_hbm,
    u_hbm,
    w_hbm,
    book_hbm,
    temper_hbm,
    input_ref,
    rotation_ref,
    codes_ref,
    x_ref,
    u_ref,
    w_ref,
    book_ref,
    temper_ref,
    turned,
    slope,
    grad,
    recon,
    cg,
    w_all,
    g_all,
    rot_sum,
    pair_out,
    pair_got,
    rest_out,
    rest_got,
    code_sum,
    code_all,
    load_sems,
    w_send,
    w_recv,
    g_send,
    g_recv,
    pair_send,
    pair_recv,
    rest_send,
    rest_recv,
    code_send,
    code_recv,
):
    row, sub = lax.axis_index("row"), lax.axis_index("sub")
    rows, features = x_ref.shape
    columns = w_ref.shape[1]
    codes = book_ref.shape[1]
    span = columns // CHUNKS
    slab = features // sub_count
    rests = row_count // 2
    bit, rest = lax.rem(row, 2), row // 2
    partner = rest * 2 + (1 - bit)
    block = features // row_count
    half = codes // 2
    piece = span // rests if share else 16

    loads = [
        pltpu.make_async_copy(src, dst, load_sems.at[i])
        for i, (src, dst) in enumerate(
            [
                (x_hbm, x_ref),
                (w_hbm, w_ref),
                (u_hbm, u_ref),
                (book_hbm, book_ref),
                (temper_hbm, temper_ref),
            ]
        )
    ]
    for load in loads:
        load.start()

    barrier = pltpu.get_barrier_semaphore()

    def greet_row(peer):
        pl.semaphore_signal(barrier, inc=1, device_id=(peer, sub), device_id_type=MESH)

    def greet_sub(peer):
        pl.semaphore_signal(barrier, inc=1, device_id=(row, peer), device_id_type=MESH)

    if share:
        for_peers(row, row_count, greet_row)
    for_peers(sub, sub_count, greet_sub)

    def remote(src, dst, send, recv, device):
        return pltpu.make_async_remote_copy(
            src_ref=src,
            dst_ref=dst,
            send_sem=send,
            recv_sem=recv,
            device_id=device,
            device_id_type=MESH,
        )

    def w_copy(peer, slot):
        at = pl.ds(pl.multiple_of(peer * slab, slab), slab)
        return remote(
            w_ref.at[at], w_all.at[slot], w_send.at[peer], w_recv.at[slot], (row, peer)
        )

    def g_copy(h, peer, slot):
        at = pl.ds(h * span, span)
        return remote(
            g_all.at[slot, at],
            g_all.at[slot, at],
            g_send.at[h, peer],
            g_recv.at[h, slot],
            (row, peer),
        )

    def pair_copy(h):
        return remote(
            pair_out.at[h, 1 - bit], pair_got.at[h], pair_send.at[h], pair_recv.at[h], (partner, sub)
        )

    def rest_copy(h, peer, slot):
        return remote(
            rest_out.at[h, peer],
            rest_got.at[h, slot],
            rest_send.at[h, peer],
            rest_recv.at[h, slot],
            (peer * 2 + bit, sub),
        )

    def code_copy(h, peer, slot):
        return remote(
            code_sum.at[h],
            code_all.at[h, slot],
            code_send.at[h, peer],
            code_recv.at[h, slot],
            (peer, sub),
        )

    def work(h):
        per = span // 8

        def body(i, carry):
            subspaces(
                h * per + i * GROUP, book_ref, temper_ref, turned, slope, grad, recon, cg
            )
            return carry

        lax.fori_loop(0, per // GROUP, body, 0)

    def send_grad(h):
        at = pl.ds(h * span, span)
        g_all[sub, at, :] = grad[at, :].astype(BF16)
        for_peers(sub, sub_count, lambda peer: g_copy(h, peer, sub).start())

    def send_pair(h):
        at = pl.ds(h * span, span)
        local = nn(g_all[sub, at, :], x_ref[...]) + nn(recon[at, :].astype(BF16), u_ref[...])
        if share:
            for peer in range(rests):
                for side in range(2):
                    start = (peer * 2 + side) * block
                    pair_out[h, side, peer] = local[:, start : start + block].astype(BF16)
            for side in range(2):
                pair_out[h, side, rests] = cg[at, side * half : (side + 1) * half].astype(BF16)
            pair_copy(h).start()
        else:
            rotation_ref[at, :] = local
            codes_ref[at, :] = cg[at, :]

    def send_rest(h):
        if share:
            pair_copy(h).wait_recv()
            for peer in range(rests):
                rest_out[h, peer, :span, :] = (
                    pair_out[h, bit, peer].astype(F32) + pair_got[h, peer].astype(F32)
                ).astype(BF16)
                at = pl.ds(peer * piece, piece)
                rest_out[h, peer, span:, :] = (
                    pair_out[h, bit, rests, at].astype(F32) + pair_got[h, rests, at].astype(F32)
                ).astype(BF16)
            for_peers(rest, rests, lambda peer: rest_copy(h, peer, rest).start())

    def finish_rest(h):
        if share:
            for_peers(rest, rests, lambda peer: rest_copy(h, rest, peer).wait_recv())
            rest_got[h, rest] = rest_out[h, rest]
            total = rest_got[h, 0, span:, :].astype(F32)
            for other in range(1, rests):
                total += rest_got[h, other, span:, :].astype(F32)
            code_sum[h] = total.astype(BF16)
            for_peers(row, row_count, lambda peer: code_copy(h, peer, row).start())
            total = rest_got[h, 0, :span, :].astype(F32)
            for other in range(1, rests):
                total += rest_got[h, other, :span, :].astype(F32)
            rot_sum[pl.ds(h * span, span), :] = total

    def finish_codes(h):
        if share:
            for_peers(row, row_count, lambda peer: code_copy(h, row, peer).wait_recv())
            code_all[h, row] = code_sum[h]
            for other in range(row_count):
                codes_ref[
                    pl.ds(h * span + other // 2 * piece, piece),
                    other % 2 * half : (other % 2 + 1) * half,
                ] = code_all[h, other].astype(F32)

    loads[0].wait()
    loads[1].wait()
    turned[...] = nn(x_ref[...], w_ref[...]).T
    loads[2].wait()
    slope[...] = nn(u_ref[...], w_ref[...]).T
    loads[3].wait()
    loads[4].wait()
    pl.semaphore_wait(barrier, sub_count - 1 + (row_count - 1 if share else 0))
    for_peers(sub, sub_count, lambda peer: w_copy(peer, sub).start())

    for h in range(CHUNKS):
        work(h)
        send_grad(h)
        send_pair(h)
        if h >= 1:
            send_rest(h - 1)
        if h >= 2:
            finish_rest(h - 2)
    send_rest(CHUNKS - 1)
    finish_rest(CHUNKS - 2)

    for_peers(sub, sub_count, lambda peer: w_copy(sub, peer).wait_recv())
    w_all[sub] = w_ref[pl.ds(pl.multiple_of(sub * slab, slab), slab), :]
    for h in range(CHUNKS):
        for_peers(sub, sub_count, lambda peer: g_copy(h, sub, peer).wait_recv())
    total = nn(w_all[0], g_all[0]).astype(BF16).astype(F32)
    for other in range(1, sub_count):
        total += nn(w_all[other], g_all[other]).astype(BF16).astype(F32)
    input_ref[...] = total.T.astype(BF16)

    finish_rest(CHUNKS - 1)
    if share:
        rotation_ref[...] = rot_sum[...].T
    for h in range(CHUNKS):
        finish_codes(h)

    for_peers(sub, sub_count, lambda peer: w_copy(peer, sub).wait_send())
    for h in range(CHUNKS):
        for_peers(sub, sub_count, lambda peer: g_copy(h, peer, sub).wait_send())
        if share:
            pair_copy(h).wait_send()
            for_peers(rest, rests, lambda peer: rest_copy(h, peer, rest).wait_send())
            for_peers(row, row_count, lambda peer: code_copy(h, peer, row).wait_send())


def store_kernel(a_ref, b_ref, c_ref, a_out, b_out, c_out, sems):
    stores = [
        pltpu.make_async_copy(src, dst, sems.at[i])
        for i, (src, dst) in enumerate([(a_ref, a_out), (b_ref, b_out), (c_ref, c_out)])
    ]
    for store in stores:
        store.start()
    for store in stores:
        store.wait()


def on_device(
    feature_vectors, upstream_sensitivity, linear_mapping_matrix, centroid_tables, softness_factor
):
    row_count, sub_count = lax.axis_size("row"), lax.axis_size("sub")
    rows, features = feature_vectors.shape
    columns = linear_mapping_matrix.shape[1]
    subs, width, codes = centroid_tables.shape
    span = columns // CHUNKS
    block = features // row_count
    slab = features // sub_count
    rests = row_count // 2
    share = (
        row_count % 2 == 0
        and row_count <= 8
        and block == codes // 2
        and block % 128 == 0
        and span % (16 * rests) == 0
    )
    pieces = rests if share else 1
    piece = span // pieces
    lanes = block if share else 128
    dma = pltpu.SemaphoreType.DMA
    vmem = pl.BlockSpec(memory_space=pltpu.VMEM)
    hbm = pl.BlockSpec(memory_space=pltpu.HBM)
    rotation_shape = (block, columns) if share else (columns, features)
    results = pl.pallas_call(
        functools.partial(kernel, row_count, sub_count, share),
        out_shape=(
            jax.ShapeDtypeStruct((rows, slab), BF16),
            jax.ShapeDtypeStruct(rotation_shape, F32),
            jax.ShapeDtypeStruct((subs * width, codes), F32),
        ),
        in_specs=[hbm, hbm, hbm, hbm, hbm],
        out_specs=(vmem, vmem, vmem),
        scratch_shapes=[
            pltpu.VMEM((rows, features), BF16),
            pltpu.VMEM((rows, features), BF16),
            pltpu.VMEM((features, columns), BF16),
            pltpu.VMEM((columns, codes), F32),
            pltpu.SMEM((subs,), F32),
            pltpu.VMEM((columns, rows), F32),
            pltpu.VMEM((columns, rows), F32),
            pltpu.VMEM((columns, rows), F32),
            pltpu.VMEM((columns, rows), F32),
            pltpu.VMEM((columns, codes), F32),
            pltpu.VMEM((sub_count, slab, columns), BF16),
            pltpu.VMEM((sub_count, columns, rows), BF16),
            pltpu.VMEM((columns, lanes), F32),
            pltpu.VMEM((CHUNKS, 2, pieces + 1, span, lanes), BF16),
            pltpu.VMEM((CHUNKS, pieces + 1, span, lanes), BF16),
            pltpu.VMEM((CHUNKS, pieces, span + piece, lanes), BF16),
            pltpu.VMEM((CHUNKS, pieces, span + piece, lanes), BF16),
            pltpu.VMEM((CHUNKS, piece, lanes), BF16),
            pltpu.VMEM((CHUNKS, row_count, piece, lanes), BF16),
            dma((5,)),
            dma((sub_count,)),
            dma((sub_count,)),
            dma((CHUNKS, sub_count)),
            dma((CHUNKS, sub_count)),
            dma((CHUNKS,)),
            dma((CHUNKS,)),
            dma((CHUNKS, pieces)),
            dma((CHUNKS, pieces)),
            dma((CHUNKS, row_count)),
            dma((CHUNKS, row_count)),
        ],
        compiler_params=pltpu.CompilerParams(
            collective_id=0, has_side_effects=True, vmem_limit_bytes=54700 * 1024
        ),
        name="soft_pq_backward",
    )(
        feature_vectors,
        upstream_sensitivity,
        linear_mapping_matrix,
        centroid_tables.reshape(subs * width, codes),
        softness_factor,
    )
    if share:
        results = pl.pallas_call(
            store_kernel,
            out_shape=tuple(jax.ShapeDtypeStruct(r.shape, r.dtype) for r in results),
            in_specs=[vmem, vmem, vmem],
            out_specs=(hbm, hbm, hbm),
            scratch_shapes=[dma((3,))],
            name="store_results",
        )(*results)
        input_grad, rotation_grad, code_grad = results
    else:
        input_grad, rotation_grad, code_grad = results
        rotation_grad = lax.psum_scatter(rotation_grad.T, "row", scatter_dimension=0, tiled=True)
        code_grad = lax.psum(code_grad, "row")
    return input_grad, rotation_grad, code_grad.reshape(subs, width, codes)


def solution(mesh):
    return jax.shard_map(
        on_device,
        mesh=mesh,
        in_specs=(P("row", None), P("row", None), P(None, "sub"), P("sub", None, None), P("sub")),
        out_specs=(P("row", "sub"), P("row", "sub"), P("sub", None, None)),
        check_vma=False,
    )
```

```python
import functools

import jax
import jax.numpy as jnp
from jax import lax
from jax.experimental import pallas as pl
from jax.experimental.pallas import tpu as pltpu
from jax.sharding import PartitionSpec as P

MESH = pl.DeviceIdType.MESH
LOG2E = 1.4426950408889634
CHUNKS = 4
GROUP = 4
F32 = jnp.float32
BF16 = jnp.bfloat16


def nn(a, b):
    return lax.dot_general(a, b, (((1,), (0,)), ((), ())), preferred_element_type=F32)


def nt(a, b):
    return lax.dot_general(a, b, (((1,), (1,)), ((), ())), preferred_element_type=F32)


def low(x):
    return x.astype(BF16).astype(F32)


def split3(x):
    first = low(x)
    rest = x - first
    second = low(rest)
    return first, second, low(rest - second)


def split2(x):
    first = low(x)
    return first, low(x - first)


def for_peers(me, count, body):
    if count <= 8:
        for step in range(1, count):
            body(lax.rem(me + step, count))
    else:

        def run(step, carry):
            body(lax.rem(me + step, count))
            return carry

        lax.fori_loop(1, count, run, 0)


def subspaces(first, book_ref, temper_ref, turned_ref, slope_ref, grad_ref, recon_ref, cg_ref):
    width = 8
    codes = book_ref.shape[1]
    rows = turned_ref.shape[1]
    at = [pl.ds(pl.multiple_of((first + j) * width, width), width) for j in range(GROUP)]
    sub_k = lax.broadcasted_iota(jnp.int32, (width, codes), 0)
    sub_n = lax.broadcasted_iota(jnp.int32, (width, rows), 0)
    none_k = jnp.zeros((width, codes), F32)
    none_n = jnp.zeros((width, rows), F32)
    ones_n = jnp.where(sub_n < 3, 1.0, 0.0).astype(F32)
    one_k = jnp.where(sub_k == 0, 1.0, 0.0).astype(F32)
    books, lefts, rights = [], [], []
    for j in range(GROUP):
        temper = temper_ref[first + j]
        c, z, g = book_ref[at[j], :], turned_ref[at[j], :], slope_ref[at[j], :]
        c1, c2, c3 = split3(c)
        square = jnp.sum(c * c, 0, keepdims=True) * (-LOG2E / jnp.full((1, codes), temper, F32))
        q1, q2, q3 = split3(square)
        squares = jnp.where(
            sub_k == 0, q1, jnp.where(sub_k == 1, q2, jnp.where(sub_k == 2, q3, 0.0))
        )
        lefts.append([c1, c2, c3, c1, c2, c1, squares, none_k])
        z1, z2, z3 = split3(z * (2.0 * LOG2E / jnp.full((1, rows), temper, F32)))
        g1, g2, g3 = split3(g)
        empty = [none_n] * 8
        for_z = [z1, z1, z1, z2, z2, z3, ones_n, none_n]
        for_g = [g1, g1, g1, g2, g2, g3, none_n, none_n]
        rights.append(
            jnp.concatenate(
                [
                    jnp.concatenate(part + empty if j % 2 == 0 else empty + part, 0).astype(BF16)
                    for part in (for_z, for_g)
                ],
                1,
            )
        )
        books.append(jnp.concatenate([c1, c2, one_k, none_k], 0).astype(BF16))
    both = []
    for j in range(0, GROUP, 2):
        left = jnp.concatenate(lefts[j] + lefts[j + 1], 0).astype(BF16).T
        both.append(nn(left, rights[j]))
        both.append(nn(left, rights[j + 1]))
    exps, exps_low = [], []
    for j in range(GROUP):
        s = both[j][:, :rows]
        e = jnp.exp2(s - jnp.max(s, 0, keepdims=True))
        exps.append(e)
        exps_low.append(e.astype(BF16))
    sums = [nn(books[j], exps_low[j]) for j in range(GROUP)]
    slopes, scales, to_assign, to_weight = [], [], [], []
    for j in range(GROUP):
        z, g = turned_ref[at[j], :], slope_ref[at[j], :]
        back = 1.0 / sums[j][16:17]
        recon = (sums[j][0:8] + sums[j][8:16]) * back
        recon_ref[at[j], :] = recon
        mean = jnp.sum(g * recon, 0, keepdims=True)
        slopes.append((exps[j] * (both[j][:, rows:] - mean)).astype(BF16))
        scale = back * (2.0 / jnp.full((1, rows), temper_ref[first + j], F32))
        scales.append(scale)
        a1, a2 = split2(g * back)
        b1, b2 = split2(z * scale)
        t1, t2 = split2(scale)
        tops = jnp.where(sub_n == 0, t1, jnp.where(sub_n == 1, t2, 0.0))
        to_assign += [a1, a2, none_n, none_n]
        to_weight += [b1, b2, tops, none_n]
    ws = [nn(books[j], slopes[j]) for j in range(GROUP)]
    assign_side = jnp.concatenate(to_assign, 0).astype(BF16).T
    weight_side = jnp.concatenate(to_weight, 0).astype(BF16).T
    owner = lax.broadcasted_iota(jnp.int32, (rows, 32 * GROUP), 1) // 32
    nothing = jnp.zeros((rows, 32 * GROUP), BF16)
    stacked = jnp.concatenate(exps_low + slopes, 1)
    weights = jnp.concatenate(
        [
            jnp.where(owner == j, side, nothing)
            for side in (assign_side, weight_side)
            for j in range(GROUP)
        ],
        0,
    )
    sides = nn(stacked, weights).T
    for j in range(GROUP):
        c, z = book_ref[at[j], :], turned_ref[at[j], :]
        total = ws[j][16:17] * scales[j]
        grad_ref[at[j], :] = (ws[j][0:8] + ws[j][8:16]) * scales[j] - z * total
        mine = sides[32 * j : 32 * j + 32]
        cg_ref[at[j], :] = mine[0:8] + mine[8:16] - c * (mine[16:17] + mine[17:18])


def kernel(
    row_count,
    sub_count,
    share,
    x_hbm,
    u_hbm,
    w_hbm,
    book_hbm,
    temper_hbm,
    input_hbm,
    rotation_hbm,
    codes_hbm,
    x_ref,
    u_ref,
    w_ref,
    book_ref,
    temper_ref,
    input_ref,
    rotation_ref,
    codes_ref,
    turned,
    slope,
    grad,
    recon,
    cg,
    w_all,
    g_all,
    rot_sum,
    pair_out,
    pair_got,
    rest_out,
    rest_got,
    code_sum,
    code_all,
    load_sems,
    store_sems,
    w_send,
    w_recv,
    g_send,
    g_recv,
    pair_send,
    pair_recv,
    rest_send,
    rest_recv,
    code_send,
    code_recv,
):
    row, sub = lax.axis_index("row"), lax.axis_index("sub")
    rows, features = x_ref.shape
    columns = w_ref.shape[1]
    codes = book_ref.shape[1]
    span = columns // CHUNKS
    slab = features // sub_count
    rests = row_count // 2
    bit, rest = lax.rem(row, 2), row // 2
    partner = rest * 2 + (1 - bit)
    block = features // row_count
    half = codes // 2
    piece = span // rests if share else 16

    loads = [
        pltpu.make_async_copy(src, dst, load_sems.at[i])
        for i, (src, dst) in enumerate(
            [
                (x_hbm, x_ref),
                (w_hbm, w_ref),
                (u_hbm, u_ref),
                (book_hbm, book_ref),
                (temper_hbm, temper_ref),
            ]
        )
    ]
    for load in loads:
        load.start()

    stores = [
        pltpu.make_async_copy(src, dst, store_sems.at[i])
        for i, (src, dst) in enumerate(
            [(input_ref, input_hbm), (rotation_ref, rotation_hbm), (codes_ref, codes_hbm)]
        )
    ]

    barrier = pltpu.get_barrier_semaphore()

    def greet_row(peer):
        pl.semaphore_signal(barrier, inc=1, device_id=(peer, sub), device_id_type=MESH)

    def greet_sub(peer):
        pl.semaphore_signal(barrier, inc=1, device_id=(row, peer), device_id_type=MESH)

    if share:
        for_peers(row, row_count, greet_row)
    for_peers(sub, sub_count, greet_sub)

    def remote(src, dst, send, recv, device):
        return pltpu.make_async_remote_copy(
            src_ref=src,
            dst_ref=dst,
            send_sem=send,
            recv_sem=recv,
            device_id=device,
            device_id_type=MESH,
        )

    def w_copy(peer, slot):
        at = pl.ds(pl.multiple_of(peer * slab, slab), slab)
        return remote(
            w_ref.at[at], w_all.at[slot], w_send.at[peer], w_recv.at[slot], (row, peer)
        )

    def g_copy(h, peer, slot):
        at = pl.ds(pl.multiple_of(h * span, span), span)
        return remote(
            g_all.at[slot, at],
            g_all.at[slot, at],
            g_send.at[h, peer],
            g_recv.at[h, slot],
            (row, peer),
        )

    def pair_copy(h):
        return remote(
            pair_out.at[h, 1 - bit], pair_got.at[h], pair_send.at[h], pair_recv.at[h], (partner, sub)
        )

    def rest_copy(h, peer, slot):
        return remote(
            rest_out.at[h, peer],
            rest_got.at[h, slot],
            rest_send.at[h, peer],
            rest_recv.at[h, slot],
            (peer * 2 + bit, sub),
        )

    def code_copy(h, peer, slot):
        return remote(
            code_sum.at[h],
            code_all.at[h, slot],
            code_send.at[h, peer],
            code_recv.at[h, slot],
            (peer, sub),
        )

    def work(h):
        per = span // 8

        def body(i, carry):
            subspaces(
                h * per + i * GROUP, book_ref, temper_ref, turned, slope, grad, recon, cg
            )
            return carry

        lax.fori_loop(0, per // GROUP, body, 0)

    def send_grad(h):
        at = pl.ds(pl.multiple_of(h * span, span), span)
        g_all[sub, at, :] = grad[at, :].astype(BF16)
        for_peers(sub, sub_count, lambda peer: g_copy(h, peer, sub).start())

    def send_pair(h):
        at = pl.ds(pl.multiple_of(h * span, span), span)
        local = nn(g_all[sub, at, :], x_ref[...]) + nn(recon[at, :].astype(BF16), u_ref[...])
        if share:
            for peer in range(rests):
                for side in range(2):
                    start = (peer * 2 + side) * block
                    pair_out[h, side, peer] = local[:, start : start + block].astype(BF16)
            for side in range(2):
                pair_out[h, side, rests] = cg[at, side * half : (side + 1) * half].astype(BF16)
            pair_copy(h).start()
        else:
            rotation_ref[at, :] = local
            codes_ref[at, :] = cg[at, :]

    def send_rest(h):
        if share:
            pair_copy(h).wait_recv()
            for peer in range(rests):
                rest_out[h, peer, :span, :] = (
                    pair_out[h, bit, peer].astype(F32) + pair_got[h, peer].astype(F32)
                ).astype(BF16)
                at = pl.ds(peer * piece, piece)
                rest_out[h, peer, span:, :] = (
                    pair_out[h, bit, rests, at].astype(F32) + pair_got[h, rests, at].astype(F32)
                ).astype(BF16)
            for_peers(rest, rests, lambda peer: rest_copy(h, peer, rest).start())

    def finish_rest(h):
        if share:
            for_peers(rest, rests, lambda peer: rest_copy(h, rest, peer).wait_recv())
            rest_got[h, rest] = rest_out[h, rest]
            total = rest_got[h, 0, span:, :].astype(F32)
            for other in range(1, rests):
                total += rest_got[h, other, span:, :].astype(F32)
            code_sum[h] = total.astype(BF16)
            for_peers(row, row_count, lambda peer: code_copy(h, peer, row).start())
            total = rest_got[h, 0, :span, :].astype(F32)
            for other in range(1, rests):
                total += rest_got[h, other, :span, :].astype(F32)
            rot_sum[pl.ds(pl.multiple_of(h * span, span), span), :] = total

    def finish_codes(h):
        if share:
            for_peers(row, row_count, lambda peer: code_copy(h, row, peer).wait_recv())
            code_all[h, row] = code_sum[h]
            for other in range(row_count):
                codes_ref[
                    pl.ds(h * span + other // 2 * piece, piece),
                    other % 2 * half : (other % 2 + 1) * half,
                ] = code_all[h, other].astype(F32)

    loads[0].wait()
    loads[1].wait()
    turned[...] = nn(x_ref[...], w_ref[...]).T
    loads[2].wait()
    slope[...] = nn(u_ref[...], w_ref[...]).T
    loads[3].wait()
    loads[4].wait()
    pl.semaphore_wait(barrier, sub_count - 1 + (row_count - 1 if share else 0))
    for_peers(sub, sub_count, lambda peer: w_copy(peer, sub).start())

    def chunk(h, carry):
        work(h)
        send_grad(h)
        send_pair(h)
        pl.when(h >= 1)(lambda: send_rest(h - 1))
        pl.when(h >= 2)(lambda: finish_rest(h - 2))
        return carry

    lax.fori_loop(0, CHUNKS, chunk, 0)
    send_rest(CHUNKS - 1)
    finish_rest(CHUNKS - 2)

    for_peers(sub, sub_count, lambda peer: w_copy(sub, peer).wait_recv())
    w_all[sub] = w_ref[pl.ds(pl.multiple_of(sub * slab, slab), slab), :]
    for h in range(CHUNKS):
        for_peers(sub, sub_count, lambda peer: g_copy(h, sub, peer).wait_recv())
    total = nn(w_all[0], g_all[0]).astype(BF16).astype(F32)
    for other in range(1, sub_count):
        total += nn(w_all[other], g_all[other]).astype(BF16).astype(F32)
    input_ref[...] = total.T.astype(BF16)
    stores[0].start()

    finish_rest(CHUNKS - 1)
    if share:
        rotation_ref[...] = rot_sum[...].T
    stores[1].start()
    for h in range(CHUNKS):
        finish_codes(h)
    stores[2].start()

    for_peers(sub, sub_count, lambda peer: w_copy(peer, sub).wait_send())
    for h in range(CHUNKS):
        for_peers(sub, sub_count, lambda peer: g_copy(h, peer, sub).wait_send())
        if share:
            pair_copy(h).wait_send()
            for_peers(rest, rests, lambda peer: rest_copy(h, peer, rest).wait_send())
            for_peers(row, row_count, lambda peer: code_copy(h, peer, row).wait_send())
    for store in stores:
        store.wait()


def on_device(
    feature_vectors, upstream_sensitivity, linear_mapping_matrix, centroid_tables, softness_factor
):
    row_count, sub_count = lax.axis_size("row"), lax.axis_size("sub")
    rows, features = feature_vectors.shape
    columns = linear_mapping_matrix.shape[1]
    subs, width, codes = centroid_tables.shape
    span = columns // CHUNKS
    block = features // row_count
    slab = features // sub_count
    rests = row_count // 2
    share = (
        row_count % 2 == 0
        and row_count <= 8
        and block == codes // 2
        and block % 128 == 0
        and span % (16 * rests) == 0
    )
    pieces = rests if share else 1
    piece = span // pieces
    lanes = block if share else 128
    dma = pltpu.SemaphoreType.DMA
    hbm = pl.BlockSpec(memory_space=pltpu.HBM)
    rotation_shape = (block, columns) if share else (columns, features)
    results = pl.pallas_call(
        functools.partial(kernel, row_count, sub_count, share),
        out_shape=(
            jax.ShapeDtypeStruct((rows, slab), BF16),
            jax.ShapeDtypeStruct(rotation_shape, F32),
            jax.ShapeDtypeStruct((subs * width, codes), F32),
        ),
        in_specs=[hbm, hbm, hbm, hbm, hbm],
        out_specs=(hbm, hbm, hbm),
        scratch_shapes=[
            pltpu.VMEM((rows, features), BF16),
            pltpu.VMEM((rows, features), BF16),
            pltpu.VMEM((features, columns), BF16),
            pltpu.VMEM((columns, codes), F32),
            pltpu.SMEM((subs,), F32),
            pltpu.VMEM((rows, slab), BF16),
            pltpu.VMEM(rotation_shape, F32),
            pltpu.VMEM((subs * width, codes), F32),
            pltpu.VMEM((columns, rows), F32),
            pltpu.VMEM((columns, rows), F32),
            pltpu.VMEM((columns, rows), F32),
            pltpu.VMEM((columns, rows), F32),
            pltpu.VMEM((columns, codes), F32),
            pltpu.VMEM((sub_count, slab, columns), BF16),
            pltpu.VMEM((sub_count, columns, rows), BF16),
            pltpu.VMEM((columns, lanes), F32),
            pltpu.VMEM((CHUNKS, 2, pieces + 1, span, lanes), BF16),
            pltpu.VMEM((CHUNKS, pieces + 1, span, lanes), BF16),
            pltpu.VMEM((CHUNKS, pieces, span + piece, lanes), BF16),
            pltpu.VMEM((CHUNKS, pieces, span + piece, lanes), BF16),
            pltpu.VMEM((CHUNKS, piece, lanes), BF16),
            pltpu.VMEM((CHUNKS, row_count, piece, lanes), BF16),
            dma((5,)),
            dma((3,)),
            dma((sub_count,)),
            dma((sub_count,)),
            dma((CHUNKS, sub_count)),
            dma((CHUNKS, sub_count)),
            dma((CHUNKS,)),
            dma((CHUNKS,)),
            dma((CHUNKS, pieces)),
            dma((CHUNKS, pieces)),
            dma((CHUNKS, row_count)),
            dma((CHUNKS, row_count)),
        ],
        compiler_params=pltpu.CompilerParams(
            collective_id=0, has_side_effects=True, vmem_limit_bytes=61 * 1024 * 1024
        ),
        name="soft_pq_backward",
    )(
        feature_vectors,
        upstream_sensitivity,
        linear_mapping_matrix,
        centroid_tables.reshape(subs * width, codes),
        softness_factor,
    )
    input_grad, rotation_grad, code_grad = results
    if not share:
        rotation_grad = lax.psum_scatter(rotation_grad.T, "row", scatter_dimension=0, tiled=True)
        code_grad = lax.psum(code_grad, "row")
    return input_grad, rotation_grad, code_grad.reshape(subs, width, codes)


def solution(mesh):
    return jax.shard_map(
        on_device,
        mesh=mesh,
        in_specs=(P("row", None), P("row", None), P(None, "sub"), P("sub", None, None), P("sub")),
        out_specs=(P("row", "sub"), P("row", "sub"), P("sub", None, None)),
        check_vma=False,
    )
```

```python
import functools

import jax
import jax.numpy as jnp
from jax import lax
from jax.experimental import pallas as pl
from jax.experimental.pallas import tpu as pltpu
from jax.sharding import PartitionSpec as P

MESH = pl.DeviceIdType.MESH
LOG2E = 1.4426950408889634
CHUNKS = 4
GROUP = 4
F32 = jnp.float32
BF16 = jnp.bfloat16


def nn(a, b):
    return lax.dot_general(a, b, (((1,), (0,)), ((), ())), preferred_element_type=F32)


def nt(a, b):
    return lax.dot_general(a, b, (((1,), (1,)), ((), ())), preferred_element_type=F32)


def low(x):
    return x.astype(BF16).astype(F32)


def split3(x):
    first = low(x)
    rest = x - first
    second = low(rest)
    return first, second, low(rest - second)


def split2(x):
    first = low(x)
    return first, low(x - first)


def for_peers(me, count, body):
    if count <= 8:
        for step in range(1, count):
            body(lax.rem(me + step, count))
    else:

        def run(step, carry):
            body(lax.rem(me + step, count))
            return carry

        lax.fori_loop(1, count, run, 0)


def subspaces(first, book_ref, temper_ref, turned_ref, slope_ref, grad_ref, recon_ref, cg_ref):
    width = 8
    codes = book_ref.shape[1]
    rows = turned_ref.shape[1]
    at = [pl.ds(pl.multiple_of((first + j) * width, width), width) for j in range(GROUP)]
    sub_k = lax.broadcasted_iota(jnp.int32, (width, codes), 0)
    sub_n = lax.broadcasted_iota(jnp.int32, (width, rows), 0)
    none_k = jnp.zeros((width, codes), F32)
    none_n = jnp.zeros((width, rows), F32)
    ones_n = jnp.where(sub_n < 3, 1.0, 0.0).astype(F32)
    one_k = jnp.where(sub_k == 0, 1.0, 0.0).astype(F32)
    books, lefts, rights = [], [], []
    for j in range(GROUP):
        temper = temper_ref[first + j]
        c, z, g = book_ref[at[j], :], turned_ref[at[j], :], slope_ref[at[j], :]
        c1, c2, c3 = split3(c)
        square = jnp.sum(c * c, 0, keepdims=True) * (-LOG2E / jnp.full((1, codes), temper, F32))
        q1, q2, q3 = split3(square)
        squares = jnp.where(
            sub_k == 0, q1, jnp.where(sub_k == 1, q2, jnp.where(sub_k == 2, q3, 0.0))
        )
        lefts.append([c1, c2, c3, c1, c2, c1, squares, none_k])
        z1, z2, z3 = split3(z * (2.0 * LOG2E / jnp.full((1, rows), temper, F32)))
        g1, g2, g3 = split3(g)
        empty = [none_n] * 8
        for_z = [z1, z1, z1, z2, z2, z3, ones_n, none_n]
        for_g = [g1, g1, g1, g2, g2, g3, none_n, none_n]
        rights.append(
            jnp.concatenate(
                [
                    jnp.concatenate(part + empty if j % 2 == 0 else empty + part, 0).astype(BF16)
                    for part in (for_z, for_g)
                ],
                1,
            )
        )
        books.append(jnp.concatenate([c1, c2, one_k, none_k], 0).astype(BF16))
    both = []
    for j in range(0, GROUP, 2):
        left = jnp.concatenate(lefts[j] + lefts[j + 1], 0).astype(BF16).T
        both.append(nn(left, rights[j]))
        both.append(nn(left, rights[j + 1]))
    exps_low = []
    for j in range(GROUP):
        s = both[j][:, :rows]
        exps_low.append(jnp.exp2(s - jnp.max(s, 0, keepdims=True)).astype(BF16))
    sums = [nn(books[j], exps_low[j]) for j in range(GROUP)]
    slopes, scales, to_assign, to_weight = [], [], [], []
    for j in range(GROUP):
        z, g = turned_ref[at[j], :], slope_ref[at[j], :]
        back = 1.0 / sums[j][16:17]
        recon = (sums[j][0:8] + sums[j][8:16]) * back
        recon_ref[at[j], :] = recon
        mean = jnp.sum(g * recon, 0, keepdims=True)
        slopes.append(exps_low[j] * (both[j][:, rows:] - mean).astype(BF16))
        scale = back * (2.0 / jnp.full((1, rows), temper_ref[first + j], F32))
        scales.append(scale)
        a1, a2 = split2(g * back)
        b1, b2 = split2(z * scale)
        t1, t2 = split2(scale)
        tops = jnp.where(sub_n == 0, t1, jnp.where(sub_n == 1, t2, 0.0))
        to_assign += [a1, a2, none_n, none_n]
        to_weight += [b1, b2, tops, none_n]
    ws = [nn(books[j], slopes[j]) for j in range(GROUP)]
    assign_side = jnp.concatenate(to_assign, 0).astype(BF16).T
    weight_side = jnp.concatenate(to_weight, 0).astype(BF16).T
    owner = lax.broadcasted_iota(jnp.int32, (rows, 32 * GROUP), 1) // 32
    nothing = jnp.zeros((rows, 32 * GROUP), BF16)
    stacked = jnp.concatenate(exps_low + slopes, 1)
    weights = jnp.concatenate(
        [
            jnp.where(owner == j, side, nothing)
            for side in (assign_side, weight_side)
            for j in range(GROUP)
        ],
        0,
    )
    sides = nn(stacked, weights).T
    for j in range(GROUP):
        c, z = book_ref[at[j], :], turned_ref[at[j], :]
        total = ws[j][16:17] * scales[j]
        grad_ref[at[j], :] = (ws[j][0:8] + ws[j][8:16]) * scales[j] - z * total
        mine = sides[32 * j : 32 * j + 32]
        cg_ref[at[j], :] = mine[0:8] + mine[8:16] - c * (mine[16:17] + mine[17:18])


def kernel(
    row_count,
    sub_count,
    share,
    x_hbm,
    u_hbm,
    w_hbm,
    book_hbm,
    temper_hbm,
    input_hbm,
    rotation_hbm,
    codes_hbm,
    x_ref,
    u_ref,
    w_ref,
    book_ref,
    temper_ref,
    input_ref,
    rotation_ref,
    codes_ref,
    turned,
    slope,
    grad,
    recon,
    cg,
    w_all,
    g_all,
    rot_sum,
    pair_out,
    pair_got,
    rest_out,
    rest_got,
    code_sum,
    code_all,
    load_sems,
    store_sems,
    w_send,
    w_recv,
    g_send,
    g_recv,
    pair_send,
    pair_recv,
    rest_send,
    rest_recv,
    code_send,
    code_recv,
):
    row, sub = lax.axis_index("row"), lax.axis_index("sub")
    rows, features = x_ref.shape
    columns = w_ref.shape[1]
    codes = book_ref.shape[1]
    span = columns // CHUNKS
    slab = features // sub_count
    rests = row_count // 2
    bit, rest = lax.rem(row, 2), row // 2
    partner = rest * 2 + (1 - bit)
    block = features // row_count
    half = codes // 2
    piece = span // rests if share else 16
    sibling = sub + 1 - 2 * lax.rem(sub, 2)

    loads = [
        pltpu.make_async_copy(src, dst, load_sems.at[i])
        for i, (src, dst) in enumerate(
            [
                (x_hbm, x_ref),
                (w_hbm, w_ref),
                (u_hbm, u_ref),
                (book_hbm, book_ref),
                (temper_hbm, temper_ref),
            ]
        )
    ]
    for load in loads:
        load.start()

    stores = [
        pltpu.make_async_copy(src, dst, store_sems.at[i])
        for i, (src, dst) in enumerate(
            [(input_ref, input_hbm), (rotation_ref, rotation_hbm), (codes_ref, codes_hbm)]
        )
    ]

    barrier = pltpu.get_barrier_semaphore()

    def greet_row(peer):
        pl.semaphore_signal(barrier, inc=1, device_id=(peer, sub), device_id_type=MESH)

    def greet_sub(peer):
        pl.semaphore_signal(barrier, inc=1, device_id=(row, peer), device_id_type=MESH)

    if share:
        for_peers(row, row_count, greet_row)
    for_peers(sub, sub_count, greet_sub)

    def remote(src, dst, send, recv, device):
        return pltpu.make_async_remote_copy(
            src_ref=src,
            dst_ref=dst,
            send_sem=send,
            recv_sem=recv,
            device_id=device,
            device_id_type=MESH,
        )

    def w_copy(peer, slot):
        at = pl.ds(pl.multiple_of(peer * slab, slab), slab)
        return remote(
            w_hbm.at[at], w_all.at[slot], w_send.at[peer], w_recv.at[slot], (row, peer)
        )

    def g_copy(h, way, peer, slot):
        at = pl.ds(pl.multiple_of(h * span, span), span)
        return remote(
            g_all.at[slot, at],
            g_all.at[slot, at],
            g_send.at[h, way],
            g_recv.at[h, slot],
            (row, peer),
        )

    def far_sends(h):
        return [
            g_copy(h, step - 1, lax.rem(sub + 2 * step, sub_count), sub)
            for step in range(1, sub_count // 2)
        ]

    def near_send(h):
        return g_copy(h, sub_count - 1, sibling, sub)

    def forwards(h):
        return [
            g_copy(h, sub_count // 2 + step - 1, sibling, lax.rem(sub + 2 * step, sub_count))
            for step in range(1, sub_count // 2)
        ]

    def pair_copy(h):
        return remote(
            pair_out.at[h, 1 - bit], pair_got.at[h], pair_send.at[h], pair_recv.at[h], (partner, sub)
        )

    def rest_copy(h, peer, slot):
        return remote(
            rest_out.at[h, peer],
            rest_got.at[h, slot],
            rest_send.at[h, peer],
            rest_recv.at[h, slot],
            (peer * 2 + bit, sub),
        )

    def code_copy(h, peer, slot):
        return remote(
            code_sum.at[h],
            code_all.at[h, slot],
            code_send.at[h, peer],
            code_recv.at[h, slot],
            (peer, sub),
        )

    def work(h):
        per = span // 8

        def body(i, carry):
            subspaces(
                h * per + i * GROUP, book_ref, temper_ref, turned, slope, grad, recon, cg
            )
            return carry

        lax.fori_loop(0, per // GROUP, body, 0)

    def store_grad(h):
        at = pl.ds(pl.multiple_of(h * span, span), span)
        g_all[sub, at, :] = grad[at, :].astype(BF16)

    def send_grad(h):
        for copy in far_sends(h):
            copy.start()
        near_send(h).start()

    def forward_grad(h):
        for step in range(1, sub_count // 2):
            g_copy(h, 0, sub, lax.rem(sub + 2 * step, sub_count)).wait_recv()
        for copy in forwards(h):
            copy.start()

    def send_pair(h):
        at = pl.ds(pl.multiple_of(h * span, span), span)
        local = nn(g_all[sub, at, :], x_ref[...]) + nn(recon[at, :].astype(BF16), u_ref[...])
        if share:
            for peer in range(rests):
                for side in range(2):
                    start = (peer * 2 + side) * block
                    pair_out[h, side, peer] = local[:, start : start + block].astype(BF16)
            for side in range(2):
                pair_out[h, side, rests] = cg[at, side * half : (side + 1) * half].astype(BF16)
            pair_copy(h).start()
        else:
            rotation_ref[at, :] = local
            codes_ref[at, :] = cg[at, :]

    def send_rest(h):
        if share:
            pair_copy(h).wait_recv()
            for peer in range(rests):
                rest_out[h, peer, :span, :] = (
                    pair_out[h, bit, peer].astype(F32) + pair_got[h, peer].astype(F32)
                ).astype(BF16)
                at = pl.ds(peer * piece, piece)
                rest_out[h, peer, span:, :] = (
                    pair_out[h, bit, rests, at].astype(F32) + pair_got[h, rests, at].astype(F32)
                ).astype(BF16)
            for_peers(rest, rests, lambda peer: rest_copy(h, peer, rest).start())

    def finish_rest(h):
        if share:
            for_peers(rest, rests, lambda peer: rest_copy(h, rest, peer).wait_recv())
            rest_got[h, rest] = rest_out[h, rest]
            total = rest_got[h, 0, span:, :].astype(F32)
            for other in range(1, rests):
                total += rest_got[h, other, span:, :].astype(F32)
            code_sum[h] = total.astype(BF16)
            for_peers(row, row_count, lambda peer: code_copy(h, peer, row).start())
            total = rest_got[h, 0, :span, :].astype(F32)
            for other in range(1, rests):
                total += rest_got[h, other, :span, :].astype(F32)
            rot_sum[pl.ds(pl.multiple_of(h * span, span), span), :] = total

    def finish_codes(h):
        if share:
            for_peers(row, row_count, lambda peer: code_copy(h, row, peer).wait_recv())
            code_all[h, row] = code_sum[h]
            for other in range(row_count):
                codes_ref[
                    pl.ds(h * span + other // 2 * piece, piece),
                    other % 2 * half : (other % 2 + 1) * half,
                ] = code_all[h, other].astype(F32)

    pl.semaphore_wait(barrier, sub_count - 1 + (row_count - 1 if share else 0))
    for step in range(1, sub_count // 2):
        for side in (sub, sibling):
            w_copy(lax.rem(side + 2 * step, sub_count), sub).start()
    w_copy(sibling, sub).start()
    loads[0].wait()
    loads[1].wait()
    turned[...] = nn(x_ref[...], w_ref[...]).T
    loads[2].wait()
    slope[...] = nn(u_ref[...], w_ref[...]).T
    loads[3].wait()
    loads[4].wait()

    def chunk(h, carry):
        work(h)
        store_grad(h)
        send_pair(h)
        send_grad(h)
        pl.when(h >= 1)(lambda: send_rest(h - 1))
        pl.when(h >= 1)(lambda: forward_grad(h - 1))
        pl.when(h >= 2)(lambda: finish_rest(h - 2))
        return carry

    lax.fori_loop(0, CHUNKS, chunk, 0)
    forward_grad(CHUNKS - 1)
    send_rest(CHUNKS - 1)
    finish_rest(CHUNKS - 2)

    for_peers(sub, sub_count, lambda peer: w_copy(sub, peer).wait_recv())
    w_all[sub] = w_ref[pl.ds(pl.multiple_of(sub * slab, slab), slab), :]
    for h in range(CHUNKS):
        g_copy(h, 0, sub, sibling).wait_recv()
        for step in range(1, sub_count // 2):
            g_copy(h, 0, sub, lax.rem(sibling + 2 * step, sub_count)).wait_recv()
    total = nn(w_all[0], g_all[0]).astype(BF16).astype(F32)
    for other in range(1, sub_count):
        total += nn(w_all[other], g_all[other]).astype(BF16).astype(F32)
    input_ref[...] = low(total.T)
    stores[0].start()

    finish_rest(CHUNKS - 1)
    if share:
        rotation_ref[...] = rot_sum[...].T
    stores[1].start()
    for h in range(CHUNKS):
        finish_codes(h)
    stores[2].start()

    for_peers(sub, sub_count, lambda peer: w_copy(peer, sub).wait_send())
    for h in range(CHUNKS):
        for copy in far_sends(h) + [near_send(h)] + forwards(h):
            copy.wait_send()
        if share:
            pair_copy(h).wait_send()
            for_peers(rest, rests, lambda peer: rest_copy(h, peer, rest).wait_send())
            for_peers(row, row_count, lambda peer: code_copy(h, peer, row).wait_send())
    for store in stores:
        store.wait()


def on_device(
    feature_vectors, upstream_sensitivity, linear_mapping_matrix, centroid_tables, softness_factor
):
    row_count, sub_count = lax.axis_size("row"), lax.axis_size("sub")
    rows, features = feature_vectors.shape
    columns = linear_mapping_matrix.shape[1]
    subs, width, codes = centroid_tables.shape
    span = columns // CHUNKS
    block = features // row_count
    slab = features // sub_count
    rests = row_count // 2
    share = (
        row_count % 2 == 0
        and row_count <= 8
        and block == codes // 2
        and block % 128 == 0
        and span % (16 * rests) == 0
    )
    pieces = rests if share else 1
    piece = span // pieces
    lanes = block if share else 128
    dma = pltpu.SemaphoreType.DMA
    hbm = pl.BlockSpec(memory_space=pltpu.HBM)
    rotation_shape = (block, columns) if share else (columns, features)
    results = pl.pallas_call(
        functools.partial(kernel, row_count, sub_count, share),
        out_shape=(
            jax.ShapeDtypeStruct((rows, slab), F32),
            jax.ShapeDtypeStruct(rotation_shape, F32),
            jax.ShapeDtypeStruct((subs * width, codes), F32),
        ),
        in_specs=[hbm, hbm, hbm, hbm, hbm],
        out_specs=(hbm, hbm, hbm),
        scratch_shapes=[
            pltpu.VMEM((rows, features), BF16),
            pltpu.VMEM((rows, features), BF16),
            pltpu.VMEM((features, columns), BF16),
            pltpu.VMEM((columns, codes), F32),
            pltpu.SMEM((subs,), F32),
            pltpu.VMEM((rows, slab), F32),
            pltpu.VMEM(rotation_shape, F32),
            pltpu.VMEM((subs * width, codes), F32),
            pltpu.VMEM((columns, rows), F32),
            pltpu.VMEM((columns, rows), F32),
            pltpu.VMEM((columns, rows), F32),
            pltpu.VMEM((columns, rows), F32),
            pltpu.VMEM((columns, codes), F32),
            pltpu.VMEM((sub_count, slab, columns), BF16),
            pltpu.VMEM((sub_count, columns, rows), BF16),
            pltpu.VMEM((columns, lanes), F32),
            pltpu.VMEM((CHUNKS, 2, pieces + 1, span, lanes), BF16),
            pltpu.VMEM((CHUNKS, pieces + 1, span, lanes), BF16),
            pltpu.VMEM((CHUNKS, pieces, span + piece, lanes), BF16),
            pltpu.VMEM((CHUNKS, pieces, span + piece, lanes), BF16),
            pltpu.VMEM((CHUNKS, piece, lanes), BF16),
            pltpu.VMEM((CHUNKS, row_count, piece, lanes), BF16),
            dma((5,)),
            dma((3,)),
            dma((sub_count,)),
            dma((sub_count,)),
            dma((CHUNKS, sub_count)),
            dma((CHUNKS, sub_count)),
            dma((CHUNKS,)),
            dma((CHUNKS,)),
            dma((CHUNKS, pieces)),
            dma((CHUNKS, pieces)),
            dma((CHUNKS, row_count)),
            dma((CHUNKS, row_count)),
        ],
        compiler_params=pltpu.CompilerParams(
            collective_id=0, has_side_effects=True, vmem_limit_bytes=61 * 1024 * 1024
        ),
        name="soft_pq_backward",
    )(
        feature_vectors,
        upstream_sensitivity,
        linear_mapping_matrix,
        centroid_tables.reshape(subs * width, codes),
        softness_factor,
    )
    input_grad, rotation_grad, code_grad = results
    if not share:
        rotation_grad = lax.psum_scatter(rotation_grad.T, "row", scatter_dimension=0, tiled=True)
        code_grad = lax.psum(code_grad, "row")
    return input_grad.astype(BF16), rotation_grad, code_grad.reshape(subs, width, codes)


def solution(mesh):
    return jax.shard_map(
        on_device,
        mesh=mesh,
        in_specs=(P("row", None), P("row", None), P(None, "sub"), P("sub", None, None), P("sub")),
        out_specs=(P("row", "sub"), P("row", "sub"), P("sub", None, None)),
        check_vma=False,
    )
```

```python
import functools

import jax
import jax.numpy as jnp
from jax import lax
from jax.experimental import pallas as pl
from jax.experimental.pallas import tpu as pltpu
from jax.sharding import PartitionSpec as P

MESH = pl.DeviceIdType.MESH
LOG2E = 1.4426950408889634
CHUNKS = 4
GROUP = 4
F32 = jnp.float32
BF16 = jnp.bfloat16


def nn(a, b):
    return lax.dot_general(a, b, (((1,), (0,)), ((), ())), preferred_element_type=F32)


def nt(a, b):
    return lax.dot_general(a, b, (((1,), (1,)), ((), ())), preferred_element_type=F32)


def low(x):
    return x.astype(BF16).astype(F32)


def split3(x):
    first = low(x)
    rest = x - first
    second = low(rest)
    return first, second, low(rest - second)


def split2(x):
    first = low(x)
    return first, low(x - first)


def for_peers(me, count, body):
    if count <= 8:
        for step in range(1, count):
            body(lax.rem(me + step, count))
    else:

        def run(step, carry):
            body(lax.rem(me + step, count))
            return carry

        lax.fori_loop(1, count, run, 0)


def subspaces(first, book_ref, temper_ref, turned_ref, slope_ref, grad_ref, recon_ref, cg_ref):
    width = 8
    codes = book_ref.shape[1]
    rows = turned_ref.shape[1]
    at = [pl.ds(pl.multiple_of((first + j) * width, width), width) for j in range(GROUP)]
    sub_k = lax.broadcasted_iota(jnp.int32, (width, codes), 0)
    sub_n = lax.broadcasted_iota(jnp.int32, (width, rows), 0)
    none_k = jnp.zeros((width, codes), F32)
    none_n = jnp.zeros((width, rows), F32)
    ones_n = jnp.where(sub_n < 3, 1.0, 0.0).astype(F32)
    one_k = jnp.where(sub_k == 0, 1.0, 0.0).astype(F32)
    books, lefts, rights = [], [], []
    for j in range(GROUP):
        temper = temper_ref[first + j]
        c, z, g = book_ref[at[j], :], turned_ref[at[j], :], slope_ref[at[j], :]
        c1, c2, c3 = split3(c)
        square = jnp.sum(c * c, 0, keepdims=True) * (-LOG2E / jnp.full((1, codes), temper, F32))
        q1, q2, q3 = split3(square)
        squares = jnp.where(
            sub_k == 0, q1, jnp.where(sub_k == 1, q2, jnp.where(sub_k == 2, q3, 0.0))
        )
        lefts.append([c1, c2, c3, c1, c2, c1, squares, none_k])
        z1, z2, z3 = split3(z * (2.0 * LOG2E / jnp.full((1, rows), temper, F32)))
        g1, g2, g3 = split3(g)
        empty = [none_n] * 8
        for_z = [z1, z1, z1, z2, z2, z3, ones_n, none_n]
        for_g = [g1, g1, g1, g2, g2, g3, none_n, none_n]
        rights.append(
            jnp.concatenate(
                [
                    jnp.concatenate(part + empty if j % 2 == 0 else empty + part, 0).astype(BF16)
                    for part in (for_z, for_g)
                ],
                1,
            )
        )
        books.append(jnp.concatenate([c1, c2, one_k, none_k], 0).astype(BF16))
    both = []
    for j in range(0, GROUP, 2):
        left = jnp.concatenate(lefts[j] + lefts[j + 1], 0).astype(BF16).T
        both.append(nn(left, rights[j]))
        both.append(nn(left, rights[j + 1]))
    exps, exps_low = [], []
    for j in range(GROUP):
        s = both[j][:, :rows]
        e = jnp.exp2(s - jnp.max(s, 0, keepdims=True))
        exps.append(e)
        exps_low.append(e.astype(BF16))
    sums = [nn(books[j], exps_low[j]) for j in range(GROUP)]
    slopes, scales, to_assign, to_weight = [], [], [], []
    for j in range(GROUP):
        z, g = turned_ref[at[j], :], slope_ref[at[j], :]
        back = 1.0 / sums[j][16:17]
        recon = (sums[j][0:8] + sums[j][8:16]) * back
        recon_ref[at[j], :] = recon
        mean = jnp.sum(g * recon, 0, keepdims=True)
        slopes.append((exps[j] * (both[j][:, rows:] - mean)).astype(BF16))
        scale = back * (2.0 / jnp.full((1, rows), temper_ref[first + j], F32))
        scales.append(scale)
        a1, a2 = split2(g * back)
        b1, b2 = split2(z * scale)
        t1, t2 = split2(scale)
        tops = jnp.where(sub_n == 0, t1, jnp.where(sub_n == 1, t2, 0.0))
        to_assign += [a1, a2, none_n, none_n]
        to_weight += [b1, b2, tops, none_n]
    ws = [nn(books[j], slopes[j]) for j in range(GROUP)]
    assign_side = jnp.concatenate(to_assign, 0).astype(BF16).T
    weight_side = jnp.concatenate(to_weight, 0).astype(BF16).T
    owner = lax.broadcasted_iota(jnp.int32, (rows, 32 * GROUP), 1) // 32
    nothing = jnp.zeros((rows, 32 * GROUP), BF16)
    stacked = jnp.concatenate(exps_low + slopes, 1)
    weights = jnp.concatenate(
        [
            jnp.where(owner == j, side, nothing)
            for side in (assign_side, weight_side)
            for j in range(GROUP)
        ],
        0,
    )
    sides = nn(stacked, weights).T
    for j in range(GROUP):
        c, z = book_ref[at[j], :], turned_ref[at[j], :]
        total = ws[j][16:17] * scales[j]
        grad_ref[at[j], :] = (ws[j][0:8] + ws[j][8:16]) * scales[j] - z * total
        mine = sides[32 * j : 32 * j + 32]
        cg_ref[at[j], :] = mine[0:8] + mine[8:16] - c * (mine[16:17] + mine[17:18])


def kernel(
    row_count,
    sub_count,
    share,
    x_hbm,
    u_hbm,
    w_hbm,
    book_hbm,
    temper_hbm,
    input_hbm,
    rotation_hbm,
    codes_hbm,
    x_ref,
    u_ref,
    w_ref,
    book_ref,
    temper_ref,
    input_ref,
    rotation_ref,
    codes_ref,
    turned,
    slope,
    grad,
    recon,
    cg,
    w_all,
    g_all,
    rot_sum,
    pair_out,
    pair_got,
    rest_out,
    rest_got,
    cross_out,
    cross_got,
    swap_out,
    swap_got,
    code_sum,
    code_all,
    load_sems,
    store_sems,
    w_send,
    w_recv,
    g_send,
    g_recv,
    pair_send,
    pair_recv,
    rest_send,
    rest_recv,
    cross_send,
    cross_recv,
    swap_send,
    swap_recv,
    code_send,
    code_recv,
):
    row, sub = lax.axis_index("row"), lax.axis_index("sub")
    rows, features = x_ref.shape
    columns = w_ref.shape[1]
    codes = book_ref.shape[1]
    span = columns // CHUNKS
    slab = features // sub_count
    rests = row_count // 2
    bit, rest = lax.rem(row, 2), row // 2
    partner = rest * 2 + (1 - bit)
    block = features // row_count
    half = codes // 2
    mid = span // 2
    piece = span // rests if share else 16
    sibling = sub + 1 - 2 * lax.rem(sub, 2)

    loads = [
        pltpu.make_async_copy(src, dst, load_sems.at[i])
        for i, (src, dst) in enumerate(
            [
                (x_hbm, x_ref),
                (w_hbm, w_ref),
                (u_hbm, u_ref),
                (book_hbm, book_ref),
                (temper_hbm, temper_ref),
            ]
        )
    ]
    for load in loads:
        load.start()

    stores = [
        pltpu.make_async_copy(src, dst, store_sems.at[i])
        for i, (src, dst) in enumerate(
            [(input_ref, input_hbm), (rotation_ref, rotation_hbm), (codes_ref, codes_hbm)]
        )
    ]

    barrier = pltpu.get_barrier_semaphore()

    def greet_row(peer):
        pl.semaphore_signal(barrier, inc=1, device_id=(peer, sub), device_id_type=MESH)

    def greet_sub(peer):
        pl.semaphore_signal(barrier, inc=1, device_id=(row, peer), device_id_type=MESH)

    if share:
        for_peers(row, row_count, greet_row)
    for_peers(sub, sub_count, greet_sub)

    def remote(src, dst, send, recv, device):
        return pltpu.make_async_remote_copy(
            src_ref=src,
            dst_ref=dst,
            send_sem=send,
            recv_sem=recv,
            device_id=device,
            device_id_type=MESH,
        )

    def w_copy(peer, slot):
        at = pl.ds(pl.multiple_of(peer * slab, slab), slab)
        return remote(
            w_hbm.at[at], w_all.at[slot], w_send.at[peer], w_recv.at[slot], (row, peer)
        )

    def g_copy(h, way, peer, slot):
        at = pl.ds(pl.multiple_of(h * span, span), span)
        return remote(
            g_all.at[slot, at],
            g_all.at[slot, at],
            g_send.at[h, way],
            g_recv.at[h, slot],
            (row, peer),
        )

    def far_sends(h):
        return [
            g_copy(h, step - 1, lax.rem(sub + 2 * step, sub_count), sub)
            for step in range(1, sub_count // 2)
        ]

    def near_send(h):
        return g_copy(h, sub_count - 1, sibling, sub)

    def forwards(h):
        return [
            g_copy(h, sub_count // 2 + step - 1, sibling, lax.rem(sub + 2 * step, sub_count))
            for step in range(1, sub_count // 2)
        ]

    def pair_copy(h):
        return remote(
            pair_out.at[h, 1 - bit], pair_got.at[h], pair_send.at[h], pair_recv.at[h], (partner, sub)
        )

    def rest_copy(h, peer, slot):
        return remote(
            rest_out.at[h, peer],
            rest_got.at[h, slot],
            rest_send.at[h, peer],
            rest_recv.at[h, slot],
            (peer * 2 + bit, sub),
        )

    def cross_copy(h, peer, slot):
        return remote(
            cross_out.at[h, peer],
            cross_got.at[h, slot],
            cross_send.at[h, peer],
            cross_recv.at[h, slot],
            (peer * 2 + bit, sub),
        )

    def swap_copy(h):
        return remote(
            swap_out.at[h, 1 - bit], swap_got.at[h], swap_send.at[h], swap_recv.at[h], (partner, sub)
        )

    def code_copy(h, peer, slot):
        return remote(
            code_sum.at[h],
            code_all.at[h, slot],
            code_send.at[h, peer],
            code_recv.at[h, slot],
            (peer, sub),
        )

    def work(h):
        per = span // 8

        def body(i, carry):
            subspaces(
                h * per + i * GROUP, book_ref, temper_ref, turned, slope, grad, recon, cg
            )
            return carry

        lax.fori_loop(0, per // GROUP, body, 0)

    def store_grad(h):
        at = pl.ds(pl.multiple_of(h * span, span), span)
        g_all[sub, at, :] = grad[at, :].astype(BF16)

    def send_grad(h):
        for copy in far_sends(h):
            copy.start()
        near_send(h).start()

    def forward_grad(h):
        for step in range(1, sub_count // 2):
            g_copy(h, 0, sub, lax.rem(sub + 2 * step, sub_count)).wait_recv()
        for copy in forwards(h):
            copy.start()

    def send_pair(h):
        at = pl.ds(pl.multiple_of(h * span, span), span)
        local = nn(g_all[sub, at, :], x_ref[...]) + nn(recon[at, :].astype(BF16), u_ref[...])
        if share:
            for peer in range(rests):
                codes_at = pl.ds(pl.multiple_of(h * span + peer * piece, piece), piece)
                for side in range(2):
                    start = (peer * 2 + side) * block
                    part = local[:, start : start + block].astype(BF16)
                    pair_out[h, side, peer] = part[:mid]
                    cross_out[h, peer, side, :mid, :] = part[mid:]
                    cross_out[h, peer, side, mid:, :] = cg[
                        codes_at, side * half : (side + 1) * half
                    ].astype(BF16)
            pair_copy(h).start()
            for_peers(rest, rests, lambda peer: cross_copy(h, peer, rest).start())
        else:
            rotation_ref[at, :] = local
            codes_ref[at, :] = cg[at, :]

    def send_rest(h):
        if share:
            pair_copy(h).wait_recv()
            for peer in range(rests):
                rest_out[h, peer] = (
                    pair_out[h, bit, peer].astype(F32) + pair_got[h, peer].astype(F32)
                ).astype(BF16)
            for_peers(rest, rests, lambda peer: rest_copy(h, peer, rest).start())
            for_peers(rest, rests, lambda peer: cross_copy(h, rest, peer).wait_recv())
            cross_got[h, rest] = cross_out[h, rest]
            total = cross_got[h, 0].astype(F32)
            for other in range(1, rests):
                total += cross_got[h, other].astype(F32)
            swap_out[h] = total.astype(BF16)
            swap_copy(h).start()

    def finish_rest(h):
        if share:
            swap_copy(h).wait_recv()
            total = swap_out[h, bit].astype(F32) + swap_got[h].astype(F32)
            code_sum[h] = total[mid:].astype(BF16)
            for_peers(row, row_count, lambda peer: code_copy(h, peer, row).start())
            rot_sum[pl.ds(pl.multiple_of(h * span + mid, mid), mid), :] = total[:mid]
            for_peers(rest, rests, lambda peer: rest_copy(h, rest, peer).wait_recv())
            rest_got[h, rest] = rest_out[h, rest]
            total = rest_got[h, 0].astype(F32)
            for other in range(1, rests):
                total += rest_got[h, other].astype(F32)
            rot_sum[pl.ds(pl.multiple_of(h * span, mid), mid), :] = total

    def finish_codes(h):
        if share:
            for_peers(row, row_count, lambda peer: code_copy(h, row, peer).wait_recv())
            code_all[h, row] = code_sum[h]
            for other in range(row_count):
                codes_ref[
                    pl.ds(h * span + other // 2 * piece, piece),
                    other % 2 * half : (other % 2 + 1) * half,
                ] = code_all[h, other].astype(F32)

    pl.semaphore_wait(barrier, sub_count - 1 + (row_count - 1 if share else 0))
    for step in range(1, sub_count // 2):
        for side in (sub, sibling):
            w_copy(lax.rem(side + 2 * step, sub_count), sub).start()
    w_copy(sibling, sub).start()
    loads[0].wait()
    loads[1].wait()
    turned[...] = nn(x_ref[...], w_ref[...]).T
    loads[2].wait()
    slope[...] = nn(u_ref[...], w_ref[...]).T
    loads[3].wait()
    loads[4].wait()

    def chunk(h, carry):
        work(h)
        store_grad(h)
        send_pair(h)
        send_grad(h)
        pl.when(h >= 1)(lambda: send_rest(h - 1))
        pl.when(h >= 1)(lambda: forward_grad(h - 1))
        pl.when(h >= 2)(lambda: finish_rest(h - 2))
        return carry

    lax.fori_loop(0, CHUNKS, chunk, 0)
    forward_grad(CHUNKS - 1)
    send_rest(CHUNKS - 1)
    finish_rest(CHUNKS - 2)

    for_peers(sub, sub_count, lambda peer: w_copy(sub, peer).wait_recv())
    w_all[sub] = w_ref[pl.ds(pl.multiple_of(sub * slab, slab), slab), :]
    for h in range(CHUNKS):
        g_copy(h, 0, sub, sibling).wait_recv()
        for step in range(1, sub_count // 2):
            g_copy(h, 0, sub, lax.rem(sibling + 2 * step, sub_count)).wait_recv()
    total = nn(w_all[0], g_all[0]).astype(BF16).astype(F32)
    for other in range(1, sub_count):
        total += nn(w_all[other], g_all[other]).astype(BF16).astype(F32)
    input_ref[...] = low(total.T)
    stores[0].start()

    finish_rest(CHUNKS - 1)
    if share:
        rotation_ref[...] = rot_sum[...].T
    stores[1].start()
    for h in range(CHUNKS):
        finish_codes(h)
    stores[2].start()

    for_peers(sub, sub_count, lambda peer: w_copy(peer, sub).wait_send())
    for h in range(CHUNKS):
        for copy in far_sends(h) + [near_send(h)] + forwards(h):
            copy.wait_send()
        if share:
            pair_copy(h).wait_send()
            for_peers(rest, rests, lambda peer: rest_copy(h, peer, rest).wait_send())
            for_peers(rest, rests, lambda peer: cross_copy(h, peer, rest).wait_send())
            swap_copy(h).wait_send()
            for_peers(row, row_count, lambda peer: code_copy(h, peer, row).wait_send())
    for store in stores:
        store.wait()


def on_device(
    feature_vectors, upstream_sensitivity, linear_mapping_matrix, centroid_tables, softness_factor
):
    row_count, sub_count = lax.axis_size("row"), lax.axis_size("sub")
    rows, features = feature_vectors.shape
    columns = linear_mapping_matrix.shape[1]
    subs, width, codes = centroid_tables.shape
    span = columns // CHUNKS
    block = features // row_count
    slab = features // sub_count
    rests = row_count // 2
    share = (
        row_count % 2 == 0
        and row_count <= 8
        and block == codes // 2
        and block % 128 == 0
        and span % (16 * rests) == 0
    )
    pieces = rests if share else 1
    piece = span // pieces
    mid = span // 2
    lanes = block if share else 128
    dma = pltpu.SemaphoreType.DMA
    hbm = pl.BlockSpec(memory_space=pltpu.HBM)
    rotation_shape = (block, columns) if share else (columns, features)
    results = pl.pallas_call(
        functools.partial(kernel, row_count, sub_count, share),
        out_shape=(
            jax.ShapeDtypeStruct((rows, slab), F32),
            jax.ShapeDtypeStruct(rotation_shape, F32),
            jax.ShapeDtypeStruct((subs * width, codes), F32),
        ),
        in_specs=[hbm, hbm, hbm, hbm, hbm],
        out_specs=(hbm, hbm, hbm),
        scratch_shapes=[
            pltpu.VMEM((rows, features), BF16),
            pltpu.VMEM((rows, features), BF16),
            pltpu.VMEM((features, columns), BF16),
            pltpu.VMEM((columns, codes), F32),
            pltpu.SMEM((subs,), F32),
            pltpu.VMEM((rows, slab), F32),
            pltpu.VMEM(rotation_shape, F32),
            pltpu.VMEM((subs * width, codes), F32),
            pltpu.VMEM((columns, rows), F32),
            pltpu.VMEM((columns, rows), F32),
            pltpu.VMEM((columns, rows), F32),
            pltpu.VMEM((columns, rows), F32),
            pltpu.VMEM((columns, codes), F32),
            pltpu.VMEM((sub_count, slab, columns), BF16),
            pltpu.VMEM((sub_count, columns, rows), BF16),
            pltpu.VMEM((columns, lanes), F32),
            pltpu.VMEM((CHUNKS, 2, pieces, mid, lanes), BF16),
            pltpu.VMEM((CHUNKS, pieces, mid, lanes), BF16),
            pltpu.VMEM((CHUNKS, pieces, mid, lanes), BF16),
            pltpu.VMEM((CHUNKS, pieces, mid, lanes), BF16),
            pltpu.VMEM((CHUNKS, pieces, 2, mid + piece, lanes), BF16),
            pltpu.VMEM((CHUNKS, pieces, 2, mid + piece, lanes), BF16),
            pltpu.VMEM((CHUNKS, 2, mid + piece, lanes), BF16),
            pltpu.VMEM((CHUNKS, mid + piece, lanes), BF16),
            pltpu.VMEM((CHUNKS, piece, lanes), BF16),
            pltpu.VMEM((CHUNKS, row_count, piece, lanes), BF16),
            dma((5,)),
            dma((3,)),
            dma((sub_count,)),
            dma((sub_count,)),
            dma((CHUNKS, sub_count)),
            dma((CHUNKS, sub_count)),
            dma((CHUNKS,)),
            dma((CHUNKS,)),
            dma((CHUNKS, pieces)),
            dma((CHUNKS, pieces)),
            dma((CHUNKS, pieces)),
            dma((CHUNKS, pieces)),
            dma((CHUNKS,)),
            dma((CHUNKS,)),
            dma((CHUNKS, row_count)),
            dma((CHUNKS, row_count)),
        ],
        compiler_params=pltpu.CompilerParams(
            collective_id=0, has_side_effects=True, vmem_limit_bytes=61 * 1024 * 1024
        ),
        name="soft_pq_backward",
    )(
        feature_vectors,
        upstream_sensitivity,
        linear_mapping_matrix,
        centroid_tables.reshape(subs * width, codes),
        softness_factor,
    )
    input_grad, rotation_grad, code_grad = results
    if not share:
        rotation_grad = lax.psum_scatter(rotation_grad.T, "row", scatter_dimension=0, tiled=True)
        code_grad = lax.psum(code_grad, "row")
    return input_grad.astype(BF16), rotation_grad, code_grad.reshape(subs, width, codes)


def solution(mesh):
    return jax.shard_map(
        on_device,
        mesh=mesh,
        in_specs=(P("row", None), P("row", None), P(None, "sub"), P("sub", None, None), P("sub")),
        out_specs=(P("row", "sub"), P("row", "sub"), P("sub", None, None)),
        check_vma=False,
    )
```

```python
import functools

import jax
import jax.numpy as jnp
from jax import lax
from jax.experimental import pallas as pl
from jax.experimental.pallas import tpu as pltpu
from jax.sharding import PartitionSpec as P

MESH = pl.DeviceIdType.MESH
LOG2E = 1.4426950408889634
CHUNKS = 4
GROUP = 4
F32 = jnp.float32
BF16 = jnp.bfloat16


def nn(a, b):
    return lax.dot_general(a, b, (((1,), (0,)), ((), ())), preferred_element_type=F32)


def nt(a, b):
    return lax.dot_general(a, b, (((1,), (1,)), ((), ())), preferred_element_type=F32)


def low(x):
    return x.astype(BF16).astype(F32)


def split3(x):
    first = low(x)
    rest = x - first
    second = low(rest)
    return first, second, low(rest - second)


def split2(x):
    first = low(x)
    return first, low(x - first)


def for_peers(me, count, body):
    if count <= 8:
        for step in range(1, count):
            body(lax.rem(me + step, count))
    else:

        def run(step, carry):
            body(lax.rem(me + step, count))
            return carry

        lax.fori_loop(1, count, run, 0)


def subspaces(first, book_ref, temper_ref, turned_ref, slope_ref, grad_ref, recon_ref, cg_ref):
    width = 8
    codes = book_ref.shape[1]
    rows = turned_ref.shape[1]
    at = [pl.ds(pl.multiple_of((first + j) * width, width), width) for j in range(GROUP)]
    sub_k = lax.broadcasted_iota(jnp.int32, (width, codes), 0)
    sub_n = lax.broadcasted_iota(jnp.int32, (width, rows), 0)
    none_k = jnp.zeros((width, codes), F32)
    none_n = jnp.zeros((width, rows), F32)
    ones_n = jnp.where(sub_n < 3, 1.0, 0.0).astype(F32)
    one_k = jnp.where(sub_k == 0, 1.0, 0.0).astype(F32)
    both, books = [], []
    for j in range(GROUP):
        temper = temper_ref[first + j]
        c, z, g = book_ref[at[j], :], turned_ref[at[j], :], slope_ref[at[j], :]
        c1, c2, c3 = split3(c)
        square = jnp.sum(c * c, 0, keepdims=True) * (-LOG2E / jnp.full((1, codes), temper, F32))
        q1, q2, q3 = split3(square)
        squares = jnp.where(
            sub_k == 0, q1, jnp.where(sub_k == 1, q2, jnp.where(sub_k == 2, q3, 0.0))
        )
        left = jnp.concatenate([c1, c2, c3, c1, c2, c1, squares, none_k], 0).astype(BF16).T
        z1, z2, z3 = split3(z * (2.0 * LOG2E / jnp.full((1, rows), temper, F32)))
        g1, g2, g3 = split3(g)
        right = jnp.concatenate(
            [
                jnp.concatenate([z1, z1, z1, z2, z2, z3, ones_n, none_n], 0).astype(BF16),
                jnp.concatenate([g1, g1, g1, g2, g2, g3, none_n, none_n], 0).astype(BF16),
            ],
            1,
        )
        both.append(nn(left, right))
        books.append(jnp.concatenate([c1, c2, one_k, none_k], 0).astype(BF16))
    exps, exps_low = [], []
    for j in range(GROUP):
        s = both[j][:, :rows]
        e = jnp.exp2(s - jnp.max(s, 0, keepdims=True))
        exps.append(e)
        exps_low.append(e.astype(BF16))
    sums = [nn(books[j], exps_low[j]) for j in range(GROUP)]
    slopes, scales, backs = [], [], []
    for j in range(GROUP):
        back = 1.0 / sums[j][16:17]
        recon = (sums[j][0:8] + sums[j][8:16]) * back
        recon_ref[at[j], :] = recon
        mean = jnp.sum(slope_ref[at[j], :] * recon, 0, keepdims=True)
        slopes.append((exps[j] * (both[j][:, rows:] - mean)).astype(BF16))
        backs.append(back)
        scales.append(back * (2.0 / jnp.full((1, rows), temper_ref[first + j], F32)))
    for j in range(GROUP):
        c, z, g = book_ref[at[j], :], turned_ref[at[j], :], slope_ref[at[j], :]
        w = nn(books[j], slopes[j])
        total = w[16:17] * scales[j]
        grad_ref[at[j], :] = (w[0:8] + w[8:16]) * scales[j] - z * total
        a1, a2 = split2(g * backs[j])
        b1, b2 = split2(z * scales[j])
        t1, t2 = split2(scales[j])
        tops = jnp.where(sub_n == 0, t1, jnp.where(sub_n == 1, t2, 0.0))
        from_assign = nt(jnp.concatenate([a1, a2], 0).astype(BF16), exps_low[j])
        from_weight = nt(jnp.concatenate([b1, b2, tops, none_n], 0).astype(BF16), slopes[j])
        cg_ref[at[j], :] = (
            (from_assign[0:8] + from_assign[8:16])
            + (from_weight[0:8] + from_weight[8:16])
            - c * (from_weight[16:17] + from_weight[17:18])
        )


def kernel(
    row_count,
    sub_count,
    share,
    x_hbm,
    u_hbm,
    w_hbm,
    book_hbm,
    temper_hbm,
    input_hbm,
    rotation_hbm,
    codes_hbm,
    x_ref,
    u_ref,
    w_ref,
    book_ref,
    temper_ref,
    input_ref,
    rotation_ref,
    codes_ref,
    turned,
    slope,
    grad,
    recon,
    cg,
    w_all,
    g_all,
    rot_sum,
    pair_out,
    pair_got,
    rest_out,
    rest_got,
    direct_got,
    code_sum,
    code_all,
    load_sems,
    store_sems,
    w_send,
    w_recv,
    g_send,
    g_recv,
    pair_send,
    pair_recv,
    rest_send,
    rest_recv,
    direct_send,
    direct_recv,
    code_send,
    code_recv,
):
    row, sub = lax.axis_index("row"), lax.axis_index("sub")
    rows, features = x_ref.shape
    columns = w_ref.shape[1]
    codes = book_ref.shape[1]
    span = columns // CHUNKS
    slab = features // sub_count
    rests = row_count // 2
    bit, rest = lax.rem(row, 2), row // 2
    partner = rest * 2 + (1 - bit)
    block = features // row_count
    half = codes // 2
    last = CHUNKS - 1
    piece = span // rests if share else 16

    loads = [
        pltpu.make_async_copy(src, dst, load_sems.at[i])
        for i, (src, dst) in enumerate(
            [
                (x_hbm, x_ref),
                (w_hbm, w_ref),
                (u_hbm, u_ref),
                (book_hbm, book_ref),
                (temper_hbm, temper_ref),
            ]
        )
    ]
    for load in loads:
        load.start()

    stores = [
        pltpu.make_async_copy(src, dst, store_sems.at[i])
        for i, (src, dst) in enumerate(
            [(input_ref, input_hbm), (rotation_ref, rotation_hbm), (codes_ref, codes_hbm)]
        )
    ]

    barrier = pltpu.get_barrier_semaphore()

    def greet_row(peer):
        pl.semaphore_signal(barrier, inc=1, device_id=(peer, sub), device_id_type=MESH)

    def greet_sub(peer):
        pl.semaphore_signal(barrier, inc=1, device_id=(row, peer), device_id_type=MESH)

    if share:
        for_peers(row, row_count, greet_row)
    for_peers(sub, sub_count, greet_sub)

    def remote(src, dst, send, recv, device):
        return pltpu.make_async_remote_copy(
            src_ref=src,
            dst_ref=dst,
            send_sem=send,
            recv_sem=recv,
            device_id=device,
            device_id_type=MESH,
        )

    def w_copy(peer, slot):
        at = pl.ds(pl.multiple_of(peer * slab, slab), slab)
        return remote(
            w_ref.at[at], w_all.at[slot], w_send.at[peer], w_recv.at[slot], (row, peer)
        )

    def g_copy(h, peer, slot):
        at = pl.ds(h * span, span)
        return remote(
            g_all.at[slot, at],
            g_all.at[slot, at],
            g_send.at[h, peer],
            g_recv.at[h, slot],
            (row, peer),
        )

    def pair_copy(h):
        return remote(
            pair_out.at[h, 1 - bit], pair_got.at[h], pair_send.at[h], pair_recv.at[h], (partner, sub)
        )

    def rest_copy(h, peer, slot):
        return remote(
            rest_out.at[h, peer],
            rest_got.at[h, slot],
            rest_send.at[h, peer],
            rest_recv.at[h, slot],
            (peer * 2 + bit, sub),
        )

    def direct_copy(h, peer, slot):
        return remote(
            pair_out.at[h, lax.rem(peer, 2), peer // 2],
            direct_got.at[slot],
            direct_send.at[peer],
            direct_recv.at[slot],
            (peer, sub),
        )

    def code_copy(h, peer, slot):
        return remote(
            code_sum.at[h],
            code_all.at[h, slot],
            code_send.at[h, peer],
            code_recv.at[h, slot],
            (peer, sub),
        )

    def work(h):
        per = span // 8

        def body(i, carry):
            subspaces(
                h * per + i * GROUP, book_ref, temper_ref, turned, slope, grad, recon, cg
            )
            return carry

        lax.fori_loop(0, per // GROUP, body, 0)

    def send_grad(h):
        for_peers(sub, sub_count, lambda peer: g_copy(h, peer, sub).start())

    def send_pair(h):
        at = pl.ds(h * span, span)
        g_all[sub, at, :] = grad[at, :].astype(BF16)
        local = nn(g_all[sub, at, :], x_ref[...]) + nn(recon[at, :].astype(BF16), u_ref[...])
        if share:
            for peer in range(rests):
                for side in range(2):
                    start = (peer * 2 + side) * block
                    pair_out[h, side, peer, :span, :] = local[:, start : start + block].astype(BF16)
                    pair_out[h, side, peer, span:, :] = cg[
                        pl.ds(h * span + peer * piece, piece), side * half : (side + 1) * half
                    ].astype(BF16)
            if h < last:
                pair_copy(h).start()
            else:
                for_peers(row, row_count, lambda peer: direct_copy(h, peer, row).start())
        else:
            rotation_ref[at, :] = local
            codes_ref[at, :] = cg[at, :]

    def send_rest(h):
        if share:
            pair_copy(h).wait_recv()
            for peer in range(rests):
                rest_out[h, peer] = (
                    pair_out[h, bit, peer].astype(F32) + pair_got[h, peer].astype(F32)
                ).astype(BF16)
            for_peers(rest, rests, lambda peer: rest_copy(h, peer, rest).start())

    def finish_rest(h):
        if share:
            for_peers(rest, rests, lambda peer: rest_copy(h, rest, peer).wait_recv())
            rest_got[h, rest] = rest_out[h, rest]
            total = rest_got[h, 0, span:, :].astype(F32)
            for other in range(1, rests):
                total += rest_got[h, other, span:, :].astype(F32)
            code_sum[h] = total.astype(BF16)
            for_peers(row, row_count, lambda peer: code_copy(h, peer, row).start())
            total = rest_got[h, 0, :span, :].astype(F32)
            for other in range(1, rests):
                total += rest_got[h, other, :span, :].astype(F32)
            rot_sum[pl.ds(h * span, span), :] = total

    def finish_direct(h):
        if share:
            for_peers(row, row_count, lambda peer: direct_copy(h, row, peer).wait_recv())
            direct_got[row] = pair_out[h, bit, rest]
            total = direct_got[0, span:, :].astype(F32)
            for other in range(1, row_count):
                total += direct_got[other, span:, :].astype(F32)
            code_sum[h] = total.astype(BF16)
            for_peers(row, row_count, lambda peer: code_copy(h, peer, row).start())
            total = direct_got[0, :span, :].astype(F32)
            for other in range(1, row_count):
                total += direct_got[other, :span, :].astype(F32)
            rot_sum[pl.ds(h * span, span), :] = total

    def finish_codes(h):
        if share:
            for_peers(row, row_count, lambda peer: code_copy(h, row, peer).wait_recv())
            code_all[h, row] = code_sum[h]
            for other in range(row_count):
                codes_ref[
                    pl.ds(h * span + other // 2 * piece, piece),
                    other % 2 * half : (other % 2 + 1) * half,
                ] = code_all[h, other].astype(F32)

    loads[0].wait()
    loads[1].wait()
    turned[...] = nn(x_ref[...], w_ref[...]).T
    loads[2].wait()
    slope[...] = nn(u_ref[...], w_ref[...]).T
    loads[3].wait()
    loads[4].wait()
    pl.semaphore_wait(barrier, sub_count - 1 + (row_count - 1 if share else 0))
    for_peers(sub, sub_count, lambda peer: w_copy(peer, sub).start())

    for h in range(CHUNKS):
        work(h)
        send_pair(h)
        send_grad(h)
        if h >= 1:
            send_rest(h - 1)
        if h >= 2:
            finish_rest(h - 2)
    finish_rest(last - 1)

    finish_direct(last)
    for_peers(sub, sub_count, lambda peer: w_copy(sub, peer).wait_recv())
    w_all[sub] = w_ref[pl.ds(pl.multiple_of(sub * slab, slab), slab), :]
    for h in range(CHUNKS):
        for_peers(sub, sub_count, lambda peer: g_copy(h, sub, peer).wait_recv())
    total = nn(w_all[0], g_all[0]).astype(BF16).astype(F32)
    for other in range(1, sub_count):
        total += nn(w_all[other], g_all[other]).astype(BF16).astype(F32)
    input_ref[...] = total.T.astype(BF16)
    stores[0].start()

    if share:
        rotation_ref[...] = rot_sum[...].T
    stores[1].start()
    for h in range(CHUNKS):
        finish_codes(h)
    stores[2].start()

    for_peers(sub, sub_count, lambda peer: w_copy(peer, sub).wait_send())
    for h in range(CHUNKS):
        for_peers(sub, sub_count, lambda peer: g_copy(h, peer, sub).wait_send())
        if share:
            if h < last:
                pair_copy(h).wait_send()
                for_peers(rest, rests, lambda peer: rest_copy(h, peer, rest).wait_send())
            else:
                for_peers(row, row_count, lambda peer: direct_copy(h, peer, row).wait_send())
            for_peers(row, row_count, lambda peer: code_copy(h, peer, row).wait_send())
    for store in stores:
        store.wait()


def on_device(
    feature_vectors, upstream_sensitivity, linear_mapping_matrix, centroid_tables, softness_factor
):
    row_count, sub_count = lax.axis_size("row"), lax.axis_size("sub")
    rows, features = feature_vectors.shape
    columns = linear_mapping_matrix.shape[1]
    subs, width, codes = centroid_tables.shape
    span = columns // CHUNKS
    block = features // row_count
    slab = features // sub_count
    rests = row_count // 2
    share = (
        row_count % 2 == 0
        and row_count <= 8
        and block == codes // 2
        and block % 128 == 0
        and span % (16 * rests) == 0
    )
    pieces = rests if share else 1
    piece = span // pieces
    lanes = block if share else 128
    dma = pltpu.SemaphoreType.DMA
    hbm = pl.BlockSpec(memory_space=pltpu.HBM)
    rotation_shape = (block, columns) if share else (columns, features)
    results = pl.pallas_call(
        functools.partial(kernel, row_count, sub_count, share),
        out_shape=(
            jax.ShapeDtypeStruct((rows, slab), BF16),
            jax.ShapeDtypeStruct(rotation_shape, F32),
            jax.ShapeDtypeStruct((subs * width, codes), F32),
        ),
        in_specs=[hbm, hbm, hbm, hbm, hbm],
        out_specs=(hbm, hbm, hbm),
        scratch_shapes=[
            pltpu.VMEM((rows, features), BF16),
            pltpu.VMEM((rows, features), BF16),
            pltpu.VMEM((features, columns), BF16),
            pltpu.VMEM((columns, codes), F32),
            pltpu.SMEM((subs,), F32),
            pltpu.VMEM((rows, slab), BF16),
            pltpu.VMEM(rotation_shape, F32),
            pltpu.VMEM((subs * width, codes), F32),
            pltpu.VMEM((columns, rows), F32),
            pltpu.VMEM((columns, rows), F32),
            pltpu.VMEM((columns, rows), F32),
            pltpu.VMEM((columns, rows), F32),
            pltpu.VMEM((columns, codes), F32),
            pltpu.VMEM((sub_count, slab, columns), BF16),
            pltpu.VMEM((sub_count, columns, rows), BF16),
            pltpu.VMEM((columns, lanes), F32),
            pltpu.VMEM((CHUNKS, 2, pieces, span + piece, lanes), BF16),
            pltpu.VMEM((CHUNKS, pieces, span + piece, lanes), BF16),
            pltpu.VMEM((CHUNKS, pieces, span + piece, lanes), BF16),
            pltpu.VMEM((CHUNKS, pieces, span + piece, lanes), BF16),
            pltpu.VMEM((row_count, span + piece, lanes), BF16),
            pltpu.VMEM((CHUNKS, piece, lanes), BF16),
            pltpu.VMEM((CHUNKS, row_count, piece, lanes), BF16),
            dma((5,)),
            dma((3,)),
            dma((sub_count,)),
            dma((sub_count,)),
            dma((CHUNKS, sub_count)),
            dma((CHUNKS, sub_count)),
            dma((CHUNKS,)),
            dma((CHUNKS,)),
            dma((CHUNKS, pieces)),
            dma((CHUNKS, pieces)),
            dma((row_count,)),
            dma((row_count,)),
            dma((CHUNKS, row_count)),
            dma((CHUNKS, row_count)),
        ],
        compiler_params=pltpu.CompilerParams(
            collective_id=0, has_side_effects=True, vmem_limit_bytes=61 * 1024 * 1024
        ),
        name="soft_pq_backward",
    )(
        feature_vectors,
        upstream_sensitivity,
        linear_mapping_matrix,
        centroid_tables.reshape(subs * width, codes),
        softness_factor,
    )
    input_grad, rotation_grad, code_grad = results
    if not share:
        rotation_grad = lax.psum_scatter(rotation_grad.T, "row", scatter_dimension=0, tiled=True)
        code_grad = lax.psum(code_grad, "row")
    return input_grad, rotation_grad, code_grad.reshape(subs, width, codes)


def solution(mesh):
    return jax.shard_map(
        on_device,
        mesh=mesh,
        in_specs=(P("row", None), P("row", None), P(None, "sub"), P("sub", None, None), P("sub")),
        out_specs=(P("row", "sub"), P("row", "sub"), P("sub", None, None)),
        check_vma=False,
    )
```

```python
import functools

import jax
import jax.numpy as jnp
from jax import lax
from jax.experimental import pallas as pl
from jax.experimental.pallas import tpu as pltpu
from jax.sharding import PartitionSpec as P

MESH = pl.DeviceIdType.MESH
LOG2E = 1.4426950408889634
CHUNKS = 4
GROUP = 8
F32 = jnp.float32
BF16 = jnp.bfloat16


def nn(a, b):
    return lax.dot_general(a, b, (((1,), (0,)), ((), ())), preferred_element_type=F32)


def nt(a, b):
    return lax.dot_general(a, b, (((1,), (1,)), ((), ())), preferred_element_type=F32)


def low(x):
    return x.astype(BF16).astype(F32)


def split3(x):
    first = low(x)
    rest = x - first
    second = low(rest)
    return first, second, low(rest - second)


def split2(x):
    first = low(x)
    return first, low(x - first)


def for_peers(me, count, body):
    if count <= 8:
        for step in range(1, count):
            body(lax.rem(me + step, count))
    else:

        def run(step, carry):
            body(lax.rem(me + step, count))
            return carry

        lax.fori_loop(1, count, run, 0)


def subspaces(first, book_ref, temper_ref, turned_ref, slope_ref, grad_ref, recon_ref, cg_ref):
    width = 8
    codes = book_ref.shape[1]
    rows = turned_ref.shape[1]
    at = [pl.ds(pl.multiple_of((first + j) * width, width), width) for j in range(GROUP)]
    sub_k = lax.broadcasted_iota(jnp.int32, (width, codes), 0)
    sub_n = lax.broadcasted_iota(jnp.int32, (width, rows), 0)
    none_k = jnp.zeros((width, codes), F32)
    none_n = jnp.zeros((width, rows), F32)
    ones_n = jnp.where(sub_n < 3, 1.0, 0.0).astype(F32)
    one_k = jnp.where(sub_k == 0, 1.0, 0.0).astype(F32)
    both, books = [], []
    for j in range(GROUP):
        temper = temper_ref[first + j]
        c, z, g = book_ref[at[j], :], turned_ref[at[j], :], slope_ref[at[j], :]
        c1, c2, c3 = split3(c)
        square = jnp.sum(c * c, 0, keepdims=True) * (-LOG2E / jnp.full((1, codes), temper, F32))
        q1, q2, q3 = split3(square)
        squares = jnp.where(
            sub_k == 0, q1, jnp.where(sub_k == 1, q2, jnp.where(sub_k == 2, q3, 0.0))
        )
        left = jnp.concatenate([c1, c2, c3, c1, c2, c1, squares, none_k], 0).astype(BF16).T
        z1, z2, z3 = split3(z * (2.0 * LOG2E / jnp.full((1, rows), temper, F32)))
        g1, g2, g3 = split3(g)
        right = jnp.concatenate(
            [
                jnp.concatenate([z1, z1, z1, z2, z2, z3, ones_n, none_n], 0).astype(BF16),
                jnp.concatenate([g1, g1, g1, g2, g2, g3, none_n, none_n], 0).astype(BF16),
            ],
            1,
        )
        both.append(nn(left, right))
        books.append(jnp.concatenate([c1, c2, one_k, none_k], 0).astype(BF16))
    exps, exps_low = [], []
    for j in range(GROUP):
        s = both[j][:, :rows]
        e = jnp.exp2(s - jnp.max(s, 0, keepdims=True))
        exps.append(e)
        exps_low.append(e.astype(BF16))
    sums = [nn(books[j], exps_low[j]) for j in range(GROUP)]
    slopes, scales, backs = [], [], []
    for j in range(GROUP):
        back = 1.0 / sums[j][16:17]
        recon = (sums[j][0:8] + sums[j][8:16]) * back
        recon_ref[at[j], :] = recon
        mean = jnp.sum(slope_ref[at[j], :] * recon, 0, keepdims=True)
        slopes.append((exps[j] * (both[j][:, rows:] - mean)).astype(BF16))
        backs.append(back)
        scales.append(back * (2.0 / jnp.full((1, rows), temper_ref[first + j], F32)))
    for j in range(GROUP):
        c, z, g = book_ref[at[j], :], turned_ref[at[j], :], slope_ref[at[j], :]
        w = nn(books[j], slopes[j])
        total = w[16:17] * scales[j]
        grad_ref[at[j], :] = (w[0:8] + w[8:16]) * scales[j] - z * total
        a1, a2 = split2(g * backs[j])
        b1, b2 = split2(z * scales[j])
        t1, t2 = split2(scales[j])
        tops = jnp.where(sub_n == 0, t1, jnp.where(sub_n == 1, t2, 0.0))
        from_assign = nt(jnp.concatenate([a1, a2], 0).astype(BF16), exps_low[j])
        from_weight = nt(jnp.concatenate([b1, b2, tops, none_n], 0).astype(BF16), slopes[j])
        cg_ref[at[j], :] = (
            (from_assign[0:8] + from_assign[8:16])
            + (from_weight[0:8] + from_weight[8:16])
            - c * (from_weight[16:17] + from_weight[17:18])
        )


def kernel(
    row_count,
    sub_count,
    share,
    x_hbm,
    u_hbm,
    w_hbm,
    book_hbm,
    temper_hbm,
    input_hbm,
    rotation_hbm,
    codes_hbm,
    x_ref,
    u_ref,
    w_ref,
    book_ref,
    temper_ref,
    input_ref,
    rotation_ref,
    codes_ref,
    turned,
    slope,
    grad,
    recon,
    cg,
    w_all,
    g_all,
    rot_sum,
    pair_out,
    pair_got,
    rest_out,
    rest_got,
    direct_got,
    code_sum,
    code_all,
    load_sems,
    store_sems,
    w_send,
    w_recv,
    g_send,
    g_recv,
    pair_send,
    pair_recv,
    rest_send,
    rest_recv,
    direct_send,
    direct_recv,
    code_send,
    code_recv,
):
    row, sub = lax.axis_index("row"), lax.axis_index("sub")
    rows, features = x_ref.shape
    columns = w_ref.shape[1]
    codes = book_ref.shape[1]
    span = columns // CHUNKS
    slab = features // sub_count
    rests = row_count // 2
    bit, rest = lax.rem(row, 2), row // 2
    partner = rest * 2 + (1 - bit)
    block = features // row_count
    half = codes // 2
    last = CHUNKS - 1
    piece = span // rests if share else 16

    loads = [
        pltpu.make_async_copy(src, dst, load_sems.at[i])
        for i, (src, dst) in enumerate(
            [
                (x_hbm, x_ref),
                (w_hbm, w_ref),
                (u_hbm, u_ref),
                (book_hbm, book_ref),
                (temper_hbm, temper_ref),
            ]
        )
    ]
    for load in loads:
        load.start()

    stores = [
        pltpu.make_async_copy(src, dst, store_sems.at[i])
        for i, (src, dst) in enumerate(
            [(input_ref, input_hbm), (rotation_ref, rotation_hbm), (codes_ref, codes_hbm)]
        )
    ]

    barrier = pltpu.get_barrier_semaphore()

    def greet_row(peer):
        pl.semaphore_signal(barrier, inc=1, device_id=(peer, sub), device_id_type=MESH)

    def greet_sub(peer):
        pl.semaphore_signal(barrier, inc=1, device_id=(row, peer), device_id_type=MESH)

    if share:
        for_peers(row, row_count, greet_row)
    for_peers(sub, sub_count, greet_sub)

    def remote(src, dst, send, recv, device):
        return pltpu.make_async_remote_copy(
            src_ref=src,
            dst_ref=dst,
            send_sem=send,
            recv_sem=recv,
            device_id=device,
            device_id_type=MESH,
        )

    def w_copy(peer, slot):
        at = pl.ds(pl.multiple_of(peer * slab, slab), slab)
        return remote(
            w_ref.at[at], w_all.at[slot], w_send.at[peer], w_recv.at[slot], (row, peer)
        )

    def g_copy(h, peer, slot):
        at = pl.ds(h * span, span)
        return remote(
            g_all.at[slot, at],
            g_all.at[slot, at],
            g_send.at[h, peer],
            g_recv.at[h, slot],
            (row, peer),
        )

    def pair_copy(h):
        return remote(
            pair_out.at[h, 1 - bit], pair_got.at[h], pair_send.at[h], pair_recv.at[h], (partner, sub)
        )

    def rest_copy(h, peer, slot):
        return remote(
            rest_out.at[h, peer],
            rest_got.at[h, slot],
            rest_send.at[h, peer],
            rest_recv.at[h, slot],
            (peer * 2 + bit, sub),
        )

    def direct_copy(h, peer, slot):
        return remote(
            pair_out.at[h, lax.rem(peer, 2), peer // 2],
            direct_got.at[slot],
            direct_send.at[peer],
            direct_recv.at[slot],
            (peer, sub),
        )

    def code_copy(h, peer, slot):
        return remote(
            code_sum.at[h],
            code_all.at[h, slot],
            code_send.at[h, peer],
            code_recv.at[h, slot],
            (peer, sub),
        )

    def work(h):
        per = span // 8

        def body(i, carry):
            subspaces(
                h * per + i * GROUP, book_ref, temper_ref, turned, slope, grad, recon, cg
            )
            return carry

        lax.fori_loop(0, per // GROUP, body, 0)

    def send_grad(h):
        for_peers(sub, sub_count, lambda peer: g_copy(h, peer, sub).start())

    def send_pair(h):
        at = pl.ds(h * span, span)
        g_all[sub, at, :] = grad[at, :].astype(BF16)
        local = nn(g_all[sub, at, :], x_ref[...]) + nn(recon[at, :].astype(BF16), u_ref[...])
        if share:
            for peer in range(rests):
                for side in range(2):
                    start = (peer * 2 + side) * block
                    pair_out[h, side, peer, :span, :] = local[:, start : start + block].astype(BF16)
                    pair_out[h, side, peer, span:, :] = cg[
                        pl.ds(h * span + peer * piece, piece), side * half : (side + 1) * half
                    ].astype(BF16)
            if h < last:
                pair_copy(h).start()
            else:
                for_peers(row, row_count, lambda peer: direct_copy(h, peer, row).start())
        else:
            rotation_ref[at, :] = local
            codes_ref[at, :] = cg[at, :]

    def send_rest(h):
        if share:
            pair_copy(h).wait_recv()
            for peer in range(rests):
                rest_out[h, peer] = (
                    pair_out[h, bit, peer].astype(F32) + pair_got[h, peer].astype(F32)
                ).astype(BF16)
            for_peers(rest, rests, lambda peer: rest_copy(h, peer, rest).start())

    def finish_rest(h):
        if share:
            for_peers(rest, rests, lambda peer: rest_copy(h, rest, peer).wait_recv())
            rest_got[h, rest] = rest_out[h, rest]
            total = rest_got[h, 0, span:, :].astype(F32)
            for other in range(1, rests):
                total += rest_got[h, other, span:, :].astype(F32)
            code_sum[h] = total.astype(BF16)
            for_peers(row, row_count, lambda peer: code_copy(h, peer, row).start())
            total = rest_got[h, 0, :span, :].astype(F32)
            for other in range(1, rests):
                total += rest_got[h, other, :span, :].astype(F32)
            rot_sum[pl.ds(h * span, span), :] = total

    def finish_direct(h):
        if share:
            for_peers(row, row_count, lambda peer: direct_copy(h, row, peer).wait_recv())
            direct_got[row] = pair_out[h, bit, rest]
            total = direct_got[0, span:, :].astype(F32)
            for other in range(1, row_count):
                total += direct_got[other, span:, :].astype(F32)
            code_sum[h] = total.astype(BF16)
            for_peers(row, row_count, lambda peer: code_copy(h, peer, row).start())
            total = direct_got[0, :span, :].astype(F32)
            for other in range(1, row_count):
                total += direct_got[other, :span, :].astype(F32)
            rot_sum[pl.ds(h * span, span), :] = total

    def finish_codes(h):
        if share:
            for_peers(row, row_count, lambda peer: code_copy(h, row, peer).wait_recv())
            code_all[h, row] = code_sum[h]
            for other in range(row_count):
                codes_ref[
                    pl.ds(h * span + other // 2 * piece, piece),
                    other % 2 * half : (other % 2 + 1) * half,
                ] = code_all[h, other].astype(F32)

    loads[0].wait()
    loads[1].wait()
    turned[...] = nn(x_ref[...], w_ref[...]).T
    loads[2].wait()
    slope[...] = nn(u_ref[...], w_ref[...]).T
    loads[3].wait()
    loads[4].wait()
    pl.semaphore_wait(barrier, sub_count - 1 + (row_count - 1 if share else 0))
    for_peers(sub, sub_count, lambda peer: w_copy(peer, sub).start())

    for h in range(CHUNKS):
        work(h)
        send_pair(h)
        send_grad(h)
        if h >= 1:
            send_rest(h - 1)
        if h >= 2:
            finish_rest(h - 2)
    finish_rest(last - 1)

    finish_direct(last)
    for_peers(sub, sub_count, lambda peer: w_copy(sub, peer).wait_recv())
    w_all[sub] = w_ref[pl.ds(pl.multiple_of(sub * slab, slab), slab), :]
    for h in range(CHUNKS):
        for_peers(sub, sub_count, lambda peer: g_copy(h, sub, peer).wait_recv())
    total = nn(w_all[0], g_all[0]).astype(BF16).astype(F32)
    for other in range(1, sub_count):
        total += nn(w_all[other], g_all[other]).astype(BF16).astype(F32)
    input_ref[...] = total.T.astype(BF16)
    stores[0].start()

    if share:
        rotation_ref[...] = rot_sum[...].T
    stores[1].start()
    for h in range(CHUNKS):
        finish_codes(h)
    stores[2].start()

    for_peers(sub, sub_count, lambda peer: w_copy(peer, sub).wait_send())
    for h in range(CHUNKS):
        for_peers(sub, sub_count, lambda peer: g_copy(h, peer, sub).wait_send())
        if share:
            if h < last:
                pair_copy(h).wait_send()
                for_peers(rest, rests, lambda peer: rest_copy(h, peer, rest).wait_send())
            else:
                for_peers(row, row_count, lambda peer: direct_copy(h, peer, row).wait_send())
            for_peers(row, row_count, lambda peer: code_copy(h, peer, row).wait_send())
    for store in stores:
        store.wait()


def on_device(
    feature_vectors, upstream_sensitivity, linear_mapping_matrix, centroid_tables, softness_factor
):
    row_count, sub_count = lax.axis_size("row"), lax.axis_size("sub")
    rows, features = feature_vectors.shape
    columns = linear_mapping_matrix.shape[1]
    subs, width, codes = centroid_tables.shape
    span = columns // CHUNKS
    block = features // row_count
    slab = features // sub_count
    rests = row_count // 2
    share = (
        row_count % 2 == 0
        and row_count <= 8
        and block == codes // 2
        and block % 128 == 0
        and span % (16 * rests) == 0
    )
    pieces = rests if share else 1
    piece = span // pieces
    lanes = block if share else 128
    dma = pltpu.SemaphoreType.DMA
    hbm = pl.BlockSpec(memory_space=pltpu.HBM)
    rotation_shape = (block, columns) if share else (columns, features)
    results = pl.pallas_call(
        functools.partial(kernel, row_count, sub_count, share),
        out_shape=(
            jax.ShapeDtypeStruct((rows, slab), BF16),
            jax.ShapeDtypeStruct(rotation_shape, F32),
            jax.ShapeDtypeStruct((subs * width, codes), F32),
        ),
        in_specs=[hbm, hbm, hbm, hbm, hbm],
        out_specs=(hbm, hbm, hbm),
        scratch_shapes=[
            pltpu.VMEM((rows, features), BF16),
            pltpu.VMEM((rows, features), BF16),
            pltpu.VMEM((features, columns), BF16),
            pltpu.VMEM((columns, codes), F32),
            pltpu.SMEM((subs,), F32),
            pltpu.VMEM((rows, slab), BF16),
            pltpu.VMEM(rotation_shape, F32),
            pltpu.VMEM((subs * width, codes), F32),
            pltpu.VMEM((columns, rows), F32),
            pltpu.VMEM((columns, rows), F32),
            pltpu.VMEM((columns, rows), F32),
            pltpu.VMEM((columns, rows), F32),
            pltpu.VMEM((columns, codes), F32),
            pltpu.VMEM((sub_count, slab, columns), BF16),
            pltpu.VMEM((sub_count, columns, rows), BF16),
            pltpu.VMEM((columns, lanes), F32),
            pltpu.VMEM((CHUNKS, 2, pieces, span + piece, lanes), BF16),
            pltpu.VMEM((CHUNKS, pieces, span + piece, lanes), BF16),
            pltpu.VMEM((CHUNKS, pieces, span + piece, lanes), BF16),
            pltpu.VMEM((CHUNKS, pieces, span + piece, lanes), BF16),
            pltpu.VMEM((row_count, span + piece, lanes), BF16),
            pltpu.VMEM((CHUNKS, piece, lanes), BF16),
            pltpu.VMEM((CHUNKS, row_count, piece, lanes), BF16),
            dma((5,)),
            dma((3,)),
            dma((sub_count,)),
            dma((sub_count,)),
            dma((CHUNKS, sub_count)),
            dma((CHUNKS, sub_count)),
            dma((CHUNKS,)),
            dma((CHUNKS,)),
            dma((CHUNKS, pieces)),
            dma((CHUNKS, pieces)),
            dma((row_count,)),
            dma((row_count,)),
            dma((CHUNKS, row_count)),
            dma((CHUNKS, row_count)),
        ],
        compiler_params=pltpu.CompilerParams(
            collective_id=0, has_side_effects=True, vmem_limit_bytes=61 * 1024 * 1024
        ),
        name="soft_pq_backward",
    )(
        feature_vectors,
        upstream_sensitivity,
        linear_mapping_matrix,
        centroid_tables.reshape(subs * width, codes),
        softness_factor,
    )
    input_grad, rotation_grad, code_grad = results
    if not share:
        rotation_grad = lax.psum_scatter(rotation_grad.T, "row", scatter_dimension=0, tiled=True)
        code_grad = lax.psum(code_grad, "row")
    return input_grad, rotation_grad, code_grad.reshape(subs, width, codes)


def solution(mesh):
    return jax.shard_map(
        on_device,
        mesh=mesh,
        in_specs=(P("row", None), P("row", None), P(None, "sub"), P("sub", None, None), P("sub")),
        out_specs=(P("row", "sub"), P("row", "sub"), P("sub", None, None)),
        check_vma=False,
    )
```
